256 devices in a mesh: dp: 4 (over y), expert: 64 (over x, z, core).
Axes of the slice: x: 4, y: 4, z: 8, core: 2. Of those that a mesh axis runs over, the one named last changes fastest.
Arguments:
- tokens: bfloat16 [2048, 2048], P('dp'), may hold values from -6 to 6
- picks: int32 [2048, 8, 16], P('dp'), may hold values from 0 to 16383, all different within a row
- route_weight: float32 [2048, 8, 16], P('dp'), may hold values from 0.01 to 0.2
- out_grad: bfloat16 [2048, 2048], P('dp'), may hold values from -6 to 6
- down_rows: bfloat16 [16384, 2048], P('expert'), may hold values from -6 to 6
- up_rows: bfloat16 [16384, 2048], P('expert'), may hold values from -6 to 6
- down_mom: float32 [16384, 2048], P(('expert', 'dp')), may hold values from -1.5 to 1.5
- down_var: float32 [16384, 2048], P(('expert', 'dp')), may hold values from 0.0001 to 0.01
- up_mom: float32 [16384, 2048], P(('expert', 'dp')), may hold values from -1.5 to 1.5
- up_var: float32 [16384, 2048], P(('expert', 'dp')), may hold values from 0.0001 to 0.01
Outputs:
- layer_out: bfloat16 [2048, 2048], P('dp', 'expert')
- input_grad: bfloat16 [2048, 2048], P('dp', 'expert')
- new_down: bfloat16 [16384, 2048], P(('expert', 'dp'))
- new_up: bfloat16 [16384, 2048], P(('expert', 'dp'))
The draws below stay inside these ranges and needn't reach their ends.
Inputs may be any that keep to these rules, and one draw needn't show every extreme that they name: `picks`: for each token and head the 16 picked experts are all different; the same expert may be picked by several heads of one token.
All inputs are finite; a program needn't handle non-finite values.
Results may differ from the reference program's by a relative error of at most 0.005.
Values may be sent and summed in bfloat16 or wider, within the bound.
A program may use at most 192 MiB of HBM per device.

```python
import math
import jax
import jax.numpy as jnp
from jax import lax

D = 2048
H = 8
K = 16
EXPERTS = 16384
TOKENS = 2048


def block_scale(rng, shape, split, low, high):
    gain = 1.0
    for axis_at, blocks in split:
        heights = jax.random.uniform(jax.random.fold_in(jax.random.fold_in(rng, 6), axis_at), (blocks,), jnp.float32, low / len(split), high / len(split))
        gain = gain * jnp.repeat(jnp.exp(heights), shape[axis_at] // blocks).reshape((-1,) + (1,) * (len(shape) - 1 - axis_at))
    return gain


def choose_distinct(stream_key, rows, count, top, lift):
    ranking = jax.random.permutation(jax.random.fold_in(stream_key, 1), count)
    favour = ranking
    for power in range(3):
        favour = favour * favour // count
    favour = favour * lift // count
    chance = jax.random.randint(jax.random.fold_in(stream_key, 2), (rows, count), 0, 4096) + favour
    holders = jax.random.permutation(jax.random.fold_in(stream_key, 3), rows)[jnp.arange(count) % rows]
    chance = jnp.where(jnp.arange(rows)[:, None] == holders[None, :], 1 << 14, chance)
    priority = chance * count + jnp.arange(count)
    return lax.top_k(priority.astype(jnp.int32), top)[1].astype(jnp.int32)


def gaussian(key, extent, width, reach, shards=(), kind=jnp.bfloat16):
    loudness = block_scale(key, extent, shards, -0.22, 0.18) if shards else 1.0
    entries = jax.random.normal(key, extent, jnp.float32) * width * loudness
    return jnp.minimum(jnp.maximum(entries, -reach), reach).astype(kind)


def setup_inputs(seed: int = 0) -> dict:
    key_list = jax.random.split(jax.random.key(seed), 11)
    tokens = gaussian(key_list[0], (TOKENS, D), 1.0, 6.0, ((0, 4),))
    picks = choose_distinct(key_list[1], TOKENS * H, EXPERTS, K, 16).reshape((TOKENS, H, K))
    route_weight = jnp.clip(jnp.exp(math.log(0.2) - 2.9957323 * jax.random.uniform(key_list[2], (TOKENS, H, K), jnp.float32) ** block_scale(key_list[2], (TOKENS, H, K), ((0, 4),), -0.2, 0.2)), 0.01, 0.2)
    out_grad = gaussian(key_list[3], (TOKENS, D), 1.0, 6.0, ((0, 4),))
    down_rows = gaussian(key_list[4], (EXPERTS, D), 1.0, 6.0, ((0, 64),))
    up_rows = gaussian(key_list[5], (EXPERTS, D), 1.0, 6.0, ((0, 64),))
    down_mom = gaussian(key_list[6], (EXPERTS, D), 0.1, 1.5, ((0, 256),), jnp.float32)
    down_var = jnp.clip(jnp.exp(math.log(0.01) - 4.6051702 * jax.random.uniform(key_list[7], (EXPERTS, D), jnp.float32) ** block_scale(key_list[7], (EXPERTS, D), ((0, 256),), -0.2, 0.2)), 0.0001, 0.01)
    up_mom = gaussian(key_list[8], (EXPERTS, D), 0.1, 1.5, ((0, 256),), jnp.float32)
    up_var = jnp.clip(jnp.exp(math.log(0.01) - 4.6051702 * jax.random.uniform(key_list[9], (EXPERTS, D), jnp.float32) ** block_scale(key_list[9], (EXPERTS, D), ((0, 256),), -0.2, 0.2)), 0.0001, 0.01)
    return {"tokens": tokens, "picks": picks, "route_weight": route_weight, "out_grad": out_grad, "down_rows": down_rows, "up_rows": up_rows, "down_mom": down_mom, "down_var": down_var, "up_mom": up_mom, "up_var": up_var}


gelu_root = 0.7978845608
gelu_cube = 0.044715
learn_rate = 0.05
beta_one = 0.9
beta_two = 0.999
adam_eps = 1e-08

def gelu_value(inputs):
    inner = gelu_root * (inputs + gelu_cube * inputs * inputs * inputs)
    return 0.5 * inputs * (1.0 + jnp.tanh(inner))

def gelu_slope(inputs):
    tanh_part = jnp.tanh(gelu_root * (inputs + gelu_cube * inputs * inputs * inputs))
    return 0.5 * (1.0 + tanh_part) + 0.5 * inputs * (1.0 - tanh_part * tanh_part) * gelu_root * (1.0 + 3.0 * gelu_cube * inputs * inputs)

def adam_rows(rows, moment, second, grad):
    new_moment = beta_one * moment + (1.0 - beta_one) * grad
    new_second = beta_two * second + (1.0 - beta_two) * grad * grad
    updated = rows.astype(jnp.float32) - learn_rate * new_moment / (jnp.sqrt(new_second) + adam_eps)
    return updated.astype(jnp.bfloat16)

def reference(tokens, picks, route_weight, out_grad, down_rows, up_rows, down_mom, down_var, up_mom, up_var):
    n_tok = tokens.shape[0]
    n_pick = H * K
    inv_root = 1.0 / math.sqrt(D)
    blk_size = math.gcd(n_tok, 64)
    n_blocks = n_tok // blk_size
    expert_ids = picks.reshape(n_blocks, blk_size, n_pick).astype(jnp.int32)
    pick_weight = route_weight.reshape(n_blocks, blk_size, n_pick)
    tok_blocks = tokens.reshape(n_blocks, blk_size, D)
    cot_blocks = out_grad.reshape(n_blocks, blk_size, D)
    earlier = jnp.tril(jnp.ones((n_pick, n_pick), dtype=bool), -1)

    def one_block(totals, inputs):
        grad_down, grad_up = totals
        tok_block, ids_block, wgt_block, cot_block = inputs
        repeated = ids_block[:, :, None] == ids_block[:, None, :]
        coefficient = lax.optimization_barrier(jnp.sum(jnp.where(repeated, wgt_block[:, None, :], jnp.zeros_like(wgt_block[:, None, :])), axis=2))
        first_row = jnp.logical_not(jnp.any(jnp.logical_and(repeated, earlier[None]), axis=2))
        down_pick = down_rows[ids_block].astype(jnp.float32)
        up_pick = up_rows[ids_block].astype(jnp.float32)
        tok_float = tok_block.astype(jnp.float32)
        cot_float = cot_block.astype(jnp.float32)
        score = jnp.einsum('bd,bpd->bp', tok_float, down_pick) * inv_root
        weighted = (coefficient * gelu_value(score)).astype(jnp.bfloat16)
        weighted = jnp.where(first_row, weighted, jnp.zeros_like(weighted))
        output = jnp.einsum('bp,bpd->bd', weighted.astype(jnp.float32), up_pick).astype(jnp.bfloat16)
        back = jnp.einsum('bd,bpd->bp', cot_float, up_pick)
        score_grad = (coefficient * gelu_slope(score) * back).astype(jnp.bfloat16)
        score_grad = jnp.where(first_row, score_grad, jnp.zeros_like(score_grad))
        input_grad = (jnp.einsum('bp,bpd->bd', score_grad.astype(jnp.float32), down_pick) * inv_root).astype(jnp.bfloat16)
        flat_ids = ids_block.reshape(-1)
        down_terms = (score_grad.astype(jnp.float32)[:, :, None] * tok_float[:, None, :]).reshape(-1, D) * inv_root
        up_terms = (weighted.astype(jnp.float32)[:, :, None] * cot_float[:, None, :]).reshape(-1, D)
        grad_down = grad_down.at[flat_ids].add(down_terms)
        grad_up = grad_up.at[flat_ids].add(up_terms)
        return ((grad_down, grad_up), (output, input_grad))
    start_grads = (jnp.zeros((EXPERTS, D), jnp.float32), jnp.zeros((EXPERTS, D), jnp.float32))
    (grad_down, grad_up), (outputs, in_grads) = lax.scan(one_block, start_grads, (tok_blocks, expert_ids, pick_weight, cot_blocks))
    layer_out = outputs.reshape(n_tok, D)
    input_grad = in_grads.reshape(n_tok, D)
    new_down = adam_rows(down_rows, down_mom, down_var, grad_down)
    new_up = adam_rows(up_rows, up_mom, up_var, grad_up)
    return (layer_out, input_grad, new_down, new_up)
```

```python
import functools
import math

import jax
import jax.numpy as jnp
from jax import lax
from jax.experimental import pallas as pl
from jax.experimental.pallas import tpu as pltpu
from jax.sharding import PartitionSpec as P

gelu_root = 0.7978845608
gelu_cube = 0.044715
learn_rate = 0.05
beta_one = 0.9
beta_two = 0.999
adam_eps = 1e-08

D = 2048
E = 256
T = 512
NP = 128
OWN = 64
YN, XN, ZN = 4, 4, 8
Q = 4
R = 64 // Q
C = 4
CW = 2 * D // C
INV = 1.0 / math.sqrt(D)
MESH = pl.DeviceIdType.MESH
f32 = jnp.float32
bf16 = jnp.bfloat16


def coefficient_kernel(picks_ref, weight_ref, coef_ref, key_ref):
    first = lax.axis_index("expert") * E
    key = picks_ref[...] - first
    own = jnp.logical_and(key >= 0, key < E)
    key_ref[...] = jnp.where(own, key, -1)
    rounds = jnp.max(jnp.sum(own.astype(jnp.int32), axis=0, keepdims=True))
    coef_ref[...] = jnp.zeros((E, T), f32)

    def one_round(_, last):
        keys = key_ref[...]
        now = jnp.max(jnp.where(keys < last, keys, -1), axis=0, keepdims=True)
        total = jnp.sum(
            jnp.where(keys == now, weight_ref[...], 0.0), axis=0, keepdims=True
        )
        ids = lax.broadcasted_iota(jnp.int32, (E, T), 0)
        coef_ref[...] = jnp.where(ids == now, total, coef_ref[...])
        return now

    lax.fori_loop(0, rounds, one_round, jnp.full((1, T), E, jnp.int32))


def coefficients(picks, weights):
    vmem = pl.BlockSpec(memory_space=pltpu.VMEM)
    return pl.pallas_call(
        coefficient_kernel,
        out_shape=jax.ShapeDtypeStruct((E, T), f32),
        in_specs=[vmem, vmem],
        out_specs=vmem,
        scratch_shapes=[pltpu.VMEM((NP, T), jnp.int32)],
        compiler_params=pltpu.CompilerParams(vmem_limit_bytes=16 * 1024 * 1024),
    )(picks, weights)


def main_kernel(
    tok_hbm, cot_hbm, down_hbm, up_hbm, coef_hbm, dm_hbm, dv_hbm, um_hbm, uv_hbm,
    outs_ref, new_ref,
    acts, rows, prow, ws, pws, coef, state,
    gbuf, y1, y2, xbuf, x1, x2, zsum, zrecv, fin, fpeer,
    load_sem, pair_send, pair_recv,
    y_send, y_recv, x_send, x_recv, z_send, z_recv,
):
    y = lax.axis_index("dp")
    e = lax.axis_index("expert")
    c = lax.rem(e, 2)
    z = lax.rem(e // 2, ZN)
    x = e // (2 * ZN)

    def at(xx, zz, cc):
        return (y, (xx * ZN + zz) * 2 + cc)

    sibling = at(x, z, 1 - c)
    xp, xm = lax.rem(x + 1, XN), lax.rem(x + XN - 1, XN)
    x_right, x_left = at(xp, z, c), at(xm, z, c)
    yp, ym = lax.rem(y + 1, YN), lax.rem(y + YN - 1, YN)
    y_right, y_left = (yp, e), (ym, e)
    z_peers = [lax.rem(z + k, ZN) for k in range(1, ZN)]
    xo, yo = lax.rem(x + 2, XN), lax.rem(y + 2, YN)

    loads = []
    for i, (src, dst) in enumerate((
        (down_hbm, rows.at[0]), (up_hbm, rows.at[1]),
        (tok_hbm, acts.at[0]), (cot_hbm, acts.at[1]), (coef_hbm, coef),
        (dm_hbm, state.at[0]), (dv_hbm, state.at[1]),
        (um_hbm, state.at[2]), (uv_hbm, state.at[3]),
    )):
        copy = pltpu.make_async_copy(src, dst, load_sem.at[i])
        copy.start()
        loads.append(copy)

    barrier = pltpu.get_barrier_semaphore()
    greet = [sibling, x_right, x_left, y_right, y_left]
    greet += [at(x, p, c) for p in z_peers]
    for who in greet:
        pl.semaphore_signal(barrier, inc=1, device_id=who, device_id_type=MESH)
    pl.semaphore_wait(barrier, len(greet))

    def remote(src, dst, send, recv, who):
        return pltpu.make_async_remote_copy(
            src_ref=src, dst_ref=dst, send_sem=send, recv_sem=recv,
            device_id=who, device_id_type=MESH,
        )

    loads[0].wait()
    loads[1].wait()
    send_rows = remote(rows.at[c], prow, pair_send.at[0], pair_recv.at[0], sibling)
    send_rows.start()
    loads[2].wait()
    loads[3].wait()
    loads[4].wait()

    def score_step(i, carry):
        cols = pl.ds(pl.multiple_of(i * 128, 128), 128)
        s = lax.dot_general(
            rows[0], acts[0, cols, :], (((1,), (1,)), ((), ())),
            preferred_element_type=f32,
        ) * INV
        b = lax.dot_general(
            rows[1], acts[1, cols, :], (((1,), (1,)), ((), ())),
            preferred_element_type=f32,
        )
        k = coef[:, cols]
        u = jnp.tanh(gelu_root * (s + gelu_cube * s * s * s))
        ws[1, :, cols] = (k * (0.5 * s * (1.0 + u))).astype(bf16)
        slope = 0.5 * (1.0 + u) + 0.5 * s * (1.0 - u * u) * gelu_root * (
            1.0 + 3.0 * gelu_cube * s * s
        )
        ws[0, :, cols] = (k * slope * b).astype(bf16)
        return carry

    lax.fori_loop(0, T // 128, score_step, 0)
    send_ws = remote(ws.at[c], pws, pair_send.at[1], pair_recv.at[1], sibling)
    send_ws.start()

    def y_copy(q, kind, way):
        low = (kind != 1) == (way == 0)
        who, block = (y_right, yp) if way == 0 else (y_left, ym)
        if kind == 0:
            block = yo
        half = pl.ds(0 if low else OWN // 2, OWN // 2)
        src = gbuf.at[q, block, half, :]
        dst = y1.at[way, q] if kind == 0 else y2.at[way, q, half, :]
        return remote(src, dst, y_send.at[kind, way, q], y_recv.at[kind, way, q], who)

    for q in range(C):
        a, first = divmod(q * CW, D)

        def grad_step(i, carry, a=a, first=first, q=q):
            cols = pl.multiple_of(i * 256, 256)
            g = jnp.dot(
                ws[a], acts[a, :, pl.ds(first + cols, 256)], preferred_element_type=f32
            )
            gbuf[q, :, :, pl.ds(cols, 256)] = g.astype(bf16).reshape(YN, OWN, 256)
            return carry

        lax.fori_loop(0, CW // 256, grad_step, 0)
        for kind in (0, 1):
            for way in (0, 1):
                y_copy(q, kind, way).start()

    def x_copy(q, kind, way):
        low = (kind != 1) == (way == 0)
        who, block = (x_right, xp) if way == 0 else (x_left, xm)
        if kind == 0:
            block = xo
        half = pl.ds(0 if low else ZN // 2, ZN // 2)
        src = xbuf.at[block, q, half]
        dst = x1.at[way, q] if kind == 0 else x2.at[way, q, half]
        return remote(src, dst, x_send.at[kind, way, q], x_recv.at[kind, way, q], who)

    send_rows.wait_recv()
    send_ws.wait_recv()

    def block_of(b):
        def tile(i, carry):
            cols = pl.ds(pl.multiple_of(b * 512 + i * 256, 256), 256)
            part = lax.dot_general(
                rows[1 - c, :, cols], ws[1 - c], (((0,), (0,)), ((), ())),
                preferred_element_type=f32,
            ) + lax.dot_general(
                prow[:, cols], pws[...], (((0,), (0,)), ((), ())),
                preferred_element_type=f32,
            )
            part = part.astype(bf16)
            for k in range(4):
                for q in range(Q):
                    r = k * 64 + q * R
                    xbuf[b, q, i * 4 + k] = part[r : r + R, :]
            return carry

        lax.fori_loop(0, 2, tile, 0)

    block_of(xo)
    for q in range(Q):
        x_copy(q, 0, 0).start()
        x_copy(q, 0, 1).start()
    block_of(xp)
    for q in range(Q):
        x_copy(q, 1, 0).start()
    block_of(xm)
    for q in range(Q):
        x_copy(q, 1, 1).start()
    block_of(x)

    for q in range(max(C, Q)):
        for way in (0, 1):
            if q < Q:
                x_copy(q, 0, way).wait_recv()
                block = xp if way == 0 else xm
                half = pl.ds(0 if way == 0 else ZN // 2, ZN // 2)
                mine = xbuf[block, q, half].astype(f32)
                xbuf[block, q, half] = (mine + x1[way, q].astype(f32)).astype(bf16)
                x_copy(q, 2, way).start()
            if q < C:
                y_copy(q, 0, way).wait_recv()
                block = yp if way == 0 else ym
                half = pl.ds(0 if way == 0 else OWN // 2, OWN // 2)
                mine = gbuf[q, block, half, :].astype(f32)
                gbuf[q, block, half, :] = (mine + y1[way, q].astype(f32)).astype(bf16)
                y_copy(q, 2, way).start()

    def z_copy(q, k):
        p = z_peers[k]
        return remote(
            zsum.at[q, p], zrecv.at[q, k], z_send.at[q, k], z_recv.at[q, k], at(x, p, c)
        )

    for i in range(5, 9):
        loads[i].wait()
    for q in range(max(C, Q)):
        if q < Q:
            for way in (0, 1):
                x_copy(q, 1, way).wait_recv()
                x_copy(q, 2, way).wait_recv()
            total = (
                xbuf[x, q].astype(f32) + x2[0, q].astype(f32) + x2[1, q].astype(f32)
            )
            zsum[q] = total.astype(bf16)
            for k in range(ZN - 1):
                z_copy(q, k).start()
        if q < C:
            for way in (0, 1):
                y_copy(q, 1, way).wait_recv()
                y_copy(q, 2, way).wait_recv()
            a, first = divmod(q * CW, D)

            def adam_step(i, carry, a=a, first=first, q=q):
                r = pl.ds(pl.multiple_of(i * 16, 16), 16)
                cols = pl.ds(first, CW)
                grad = (
                    gbuf[q, y, r, :].astype(f32)
                    + y2[0, q, r, :].astype(f32)
                    + y2[1, q, r, :].astype(f32)
                )
                if a == 0:
                    grad = grad * INV
                m = beta_one * state[2 * a, r, cols] + (1.0 - beta_one) * grad
                v = beta_two * state[2 * a + 1, r, cols] + (1.0 - beta_two) * grad * grad
                old = rows[a, pl.ds(pl.multiple_of(y * OWN + i * 16, 16), 16), cols]
                new = old.astype(f32) - learn_rate * m / (jnp.sqrt(v) + adam_eps)
                new_ref[a, r, cols] = new.astype(bf16)
                return carry

            lax.fori_loop(0, OWN // 16, adam_step, 0)

    scale = jnp.where(c == 1, INV, 1.0).astype(f32)
    for q in range(Q):
        total = zsum[q, z].astype(f32)
        for k in range(ZN - 1):
            z_copy(q, k).wait_recv()
            total = total + zrecv[q, k].astype(f32)
        fin[q * R // 32, pl.ds(q * R % 32, R), :] = (total * scale).astype(bf16)
    send_fin = remote(fin.at[1 - c], fpeer, pair_send.at[2], pair_recv.at[2], sibling)
    send_fin.start()
    outs_ref[1 - c] = fin[c]
    send_fin.wait_recv()
    outs_ref[c] = fpeer[...]

    send_rows.wait_send()
    send_ws.wait_send()
    send_fin.wait_send()
    for kind in range(3):
        for way in (0, 1):
            for q in range(C):
                y_copy(q, kind, way).wait_send()
            for q in range(Q):
                x_copy(q, kind, way).wait_send()
    for q in range(Q):
        for k in range(ZN - 1):
            z_copy(q, k).wait_send()


def exchange(tokens, out_grad, down_rows, up_rows, coef, dm, dv, um, uv):
    hbm = pl.BlockSpec(memory_space=pl.ANY)
    vmem = pl.BlockSpec(memory_space=pltpu.VMEM)
    dma = pltpu.SemaphoreType.DMA
    return pl.pallas_call(
        main_kernel,
        out_shape=(
            jax.ShapeDtypeStruct((2, 32, T), bf16),
            jax.ShapeDtypeStruct((2, OWN, D), bf16),
        ),
        in_specs=[hbm] * 9,
        out_specs=(vmem, vmem),
        scratch_shapes=[
            pltpu.VMEM((2, T, D), bf16),
            pltpu.VMEM((2, E, D), bf16),
            pltpu.VMEM((E, D), bf16),
            pltpu.VMEM((2, E, T), bf16),
            pltpu.VMEM((E, T), bf16),
            pltpu.VMEM((E, T), f32),
            pltpu.VMEM((4, OWN, D), f32),
            pltpu.VMEM((C, YN, OWN, CW), bf16),
            pltpu.VMEM((2, C, OWN // 2, CW), bf16),
            pltpu.VMEM((2, C, OWN, CW), bf16),
            pltpu.VMEM((XN, Q, ZN, R, T), bf16),
            pltpu.VMEM((2, Q, ZN // 2, R, T), bf16),
            pltpu.VMEM((2, Q, ZN, R, T), bf16),
            pltpu.VMEM((Q, ZN, R, T), bf16),
            pltpu.VMEM((Q, ZN - 1, R, T), bf16),
            pltpu.VMEM((2, 32, T), bf16),
            pltpu.VMEM((32, T), bf16),
            dma((9,)),
            dma((3,)),
            dma((3,)),
            dma((3, 2, C)),
            dma((3, 2, C)),
            dma((3, 2, Q)),
            dma((3, 2, Q)),
            dma((Q, ZN - 1)),
            dma((Q, ZN - 1)),
        ],
        compiler_params=pltpu.CompilerParams(
            collective_id=0, has_side_effects=True, vmem_limit_bytes=48 * 1024 * 1024
        ),
    )(tokens, out_grad, down_rows, up_rows, coef, dm, dv, um, uv)


def local(
    tokens, picks, route_weight, out_grad, down_rows, up_rows, down_mom, down_var, up_mom, up_var
):
    picks_t = picks.transpose(1, 2, 0).reshape(NP, T)
    weight_t = route_weight.transpose(1, 2, 0).reshape(NP, T)
    coef = coefficients(picks_t, weight_t)
    outs, new = exchange(
        tokens, out_grad, down_rows, up_rows, coef, down_mom, down_var, up_mom, up_var
    )
    return (outs[1].T, outs[0].T, new[0], new[1])


def solution(mesh):
    placed = (
        P("dp", None),
        P("dp", None, None),
        P("dp", None, None),
        P("dp", None),
        P("expert", None),
        P("expert", None),
        P(("expert", "dp"), None),
        P(("expert", "dp"), None),
        P(("expert", "dp"), None),
        P(("expert", "dp"), None),
    )
    return jax.shard_map(
        local,
        mesh=mesh,
        in_specs=placed,
        out_specs=(
            P("dp", "expert"),
            P("dp", "expert"),
            P(("expert", "dp"), None),
            P(("expert", "dp"), None),
        ),
        check_vma=False,
    )
```

```python
import functools
import math

import jax
import jax.numpy as jnp
from jax import lax
from jax.experimental import pallas as pl
from jax.experimental.pallas import tpu as pltpu
from jax.sharding import PartitionSpec as P

gelu_root = 0.7978845608
gelu_cube = 0.044715
learn_rate = 0.05
beta_one = 0.9
beta_two = 0.999
adam_eps = 1e-08

D = 2048
E = 256
T = 512
NP = 128
OWN = 64
YN, XN, ZN = 4, 4, 8
Q = 4
R = 64 // Q
C = 4
CW = 2 * D // C
INV = 1.0 / math.sqrt(D)
MESH = pl.DeviceIdType.MESH
f32 = jnp.float32
bf16 = jnp.bfloat16


def coefficient_kernel(
    picks_hbm, weight_hbm, down_hbm, tok_hbm, up_hbm, cot_hbm,
    coef_ref, rows_ref, acts_ref, key_ref, weight_ref, sem,
):
    loads = []
    for i, (src, dst) in enumerate((
        (picks_hbm, key_ref), (weight_hbm, weight_ref),
        (down_hbm, rows_ref.at[0]), (tok_hbm, acts_ref.at[0]),
        (up_hbm, rows_ref.at[1]), (cot_hbm, acts_ref.at[1]),
    )):
        copy = pltpu.make_async_copy(src, dst, sem.at[i])
        copy.start()
        loads.append(copy)
    coef_ref[...] = jnp.zeros((E, T), f32)
    loads[0].wait()
    first = lax.axis_index("expert") * E
    key = key_ref[...] - first
    own = jnp.logical_and(key >= 0, key < E)
    key_ref[...] = jnp.where(own, key, -1)
    rounds = jnp.max(jnp.sum(own.astype(jnp.int32), axis=0, keepdims=True))
    loads[1].wait()

    def one_round(_, last):
        keys = key_ref[...]
        now = jnp.max(jnp.where(keys < last, keys, -1), axis=0, keepdims=True)
        total = jnp.sum(
            jnp.where(keys == now, weight_ref[...], 0.0), axis=0, keepdims=True
        )
        ids = lax.broadcasted_iota(jnp.int32, (E, T), 0)
        coef_ref[...] = jnp.where(ids == now, total, coef_ref[...])
        return now

    lax.fori_loop(0, rounds, one_round, jnp.full((1, T), E, jnp.int32))
    for copy in loads[2:]:
        copy.wait()


def coefficients(picks, weights, down_rows, tokens, up_rows, out_grad):
    vmem = pl.BlockSpec(memory_space=pltpu.VMEM)
    hbm = pl.BlockSpec(memory_space=pltpu.HBM)
    return pl.pallas_call(
        coefficient_kernel,
        out_shape=(
            pltpu.VMEM((E, T), f32),
            pltpu.VMEM((2, E, D), bf16),
            pltpu.VMEM((2, T, D), bf16),
        ),
        in_specs=[hbm] * 6,
        out_specs=(vmem, vmem, vmem),
        scratch_shapes=[
            pltpu.VMEM((NP, T), jnp.int32),
            pltpu.VMEM((NP, T), f32),
            pltpu.SemaphoreType.DMA((6,)),
        ],
        compiler_params=pltpu.CompilerParams(vmem_limit_bytes=24 * 1024 * 1024),
    )(picks, weights, down_rows, tokens, up_rows, out_grad)


def main_kernel(
    coef, rows, acts, dm_hbm, dv_hbm, um_hbm, uv_hbm,
    layer_ref, input_ref, down_ref, up_ref,
    prow, ws, pws, state,
    gbuf, y1, y2, xbuf, x1, x2, zsum, zrecv, fin, fpeer,
    load_sem, pair_send, pair_recv,
    y_send, y_recv, x_send, x_recv, z_send, z_recv,
):
    y = lax.axis_index("dp")
    e = lax.axis_index("expert")
    c = lax.rem(e, 2)
    z = lax.rem(e // 2, ZN)
    x = e // (2 * ZN)

    def at(xx, zz, cc):
        return (y, (xx * ZN + zz) * 2 + cc)

    sibling = at(x, z, 1 - c)
    xp, xm = lax.rem(x + 1, XN), lax.rem(x + XN - 1, XN)
    x_right, x_left = at(xp, z, c), at(xm, z, c)
    yp, ym = lax.rem(y + 1, YN), lax.rem(y + YN - 1, YN)
    y_right, y_left = (yp, e), (ym, e)
    z_peers = [lax.rem(z + k, ZN) for k in range(1, ZN)]
    xo, yo = lax.rem(x + 2, XN), lax.rem(y + 2, YN)

    loads = []
    for i, (src, dst) in enumerate((
        (dm_hbm, state.at[0]), (dv_hbm, state.at[1]),
        (um_hbm, state.at[2]), (uv_hbm, state.at[3]),
    )):
        copy = pltpu.make_async_copy(src, dst, load_sem.at[i])
        copy.start()
        loads.append(copy)

    barrier = pltpu.get_barrier_semaphore()
    greet = [sibling, x_right, x_left, y_right, y_left]
    greet += [at(x, p, c) for p in z_peers]
    for who in greet:
        pl.semaphore_signal(barrier, inc=1, device_id=who, device_id_type=MESH)

    def remote(src, dst, send, recv, who):
        return pltpu.make_async_remote_copy(
            src_ref=src, dst_ref=dst, send_sem=send, recv_sem=recv,
            device_id=who, device_id_type=MESH,
        )

    s = lax.dot_general(
        rows[0], acts[0], (((1,), (1,)), ((), ())), preferred_element_type=f32
    ) * INV
    b = lax.dot_general(
        rows[1], acts[1], (((1,), (1,)), ((), ())), preferred_element_type=f32
    )
    k = coef[...]
    u = jnp.tanh(gelu_root * (s + gelu_cube * s * s * s))
    ws[1] = (k * (0.5 * s * (1.0 + u))).astype(bf16)
    slope = 0.5 * (1.0 + u) + 0.5 * s * (1.0 - u * u) * gelu_root * (
        1.0 + 3.0 * gelu_cube * s * s
    )
    ws[0] = (k * slope * b).astype(bf16)
    pl.semaphore_wait(barrier, len(greet))
    send_rows = remote(rows.at[c], prow, pair_send.at[0], pair_recv.at[0], sibling)
    send_rows.start()
    send_ws = remote(ws.at[c], pws, pair_send.at[1], pair_recv.at[1], sibling)
    send_ws.start()

    def y_copy(q, kind, way):
        low = (kind != 1) == (way == 0)
        who, block = (y_right, yp) if way == 0 else (y_left, ym)
        if kind == 0:
            block = yo
        half = pl.ds(0 if low else OWN // 2, OWN // 2)
        src = gbuf.at[q, block, half, :]
        dst = y1.at[way, q] if kind == 0 else y2.at[way, q, half, :]
        return remote(src, dst, y_send.at[kind, way, q], y_recv.at[kind, way, q], who)

    for q in range(C):
        a, first = divmod(q * CW, D)
        g = jnp.dot(ws[a], acts[a, :, first : first + CW], preferred_element_type=f32)
        gbuf[q] = g.astype(bf16).reshape(YN, OWN, CW)
        for kind in (0, 1):
            for way in (0, 1):
                y_copy(q, kind, way).start()

    def x_copy(q, kind, way):
        low = (kind != 1) == (way == 0)
        who, block = (x_right, xp) if way == 0 else (x_left, xm)
        if kind == 0:
            block = xo
        half = pl.ds(0 if low else ZN // 2, ZN // 2)
        src = xbuf.at[block, q, half]
        dst = x1.at[way, q] if kind == 0 else x2.at[way, q, half]
        return remote(src, dst, x_send.at[kind, way, q], x_recv.at[kind, way, q], who)

    send_rows.wait_recv()
    send_ws.wait_recv()

    def block_of(b):
        cols = pl.ds(pl.multiple_of(b * 512, 512), 512)
        part = lax.dot_general(
            rows[1 - c, :, cols], ws[1 - c], (((0,), (0,)), ((), ())),
            preferred_element_type=f32,
        ) + lax.dot_general(
            prow[:, cols], pws[...], (((0,), (0,)), ((), ())),
            preferred_element_type=f32,
        )
        part = part.astype(bf16)
        for k in range(ZN):
            for q in range(Q):
                r = k * 64 + q * R
                xbuf[b, q, k] = part[r : r + R, :]

    block_of(xo)
    for q in range(Q):
        x_copy(q, 0, 0).start()
        x_copy(q, 0, 1).start()
    block_of(xp)
    for q in range(Q):
        x_copy(q, 1, 0).start()
    block_of(xm)
    for q in range(Q):
        x_copy(q, 1, 1).start()
    block_of(x)

    for q in range(max(C, Q)):
        for way in (0, 1):
            if q < Q:
                x_copy(q, 0, way).wait_recv()
                block = xp if way == 0 else xm
                half = pl.ds(0 if way == 0 else ZN // 2, ZN // 2)
                mine = xbuf[block, q, half].astype(f32)
                xbuf[block, q, half] = (mine + x1[way, q].astype(f32)).astype(bf16)
                x_copy(q, 2, way).start()
            if q < C:
                y_copy(q, 0, way).wait_recv()
                block = yp if way == 0 else ym
                half = pl.ds(0 if way == 0 else OWN // 2, OWN // 2)
                mine = gbuf[q, block, half, :].astype(f32)
                gbuf[q, block, half, :] = (mine + y1[way, q].astype(f32)).astype(bf16)
                y_copy(q, 2, way).start()

    def z_copy(q, k):
        p = z_peers[k]
        return remote(
            zsum.at[q, p], zrecv.at[q, k], z_send.at[q, k], z_recv.at[q, k], at(x, p, c)
        )

    for copy in loads:
        copy.wait()
    for q in range(max(C, Q)):
        if q < Q:
            for way in (0, 1):
                x_copy(q, 1, way).wait_recv()
                x_copy(q, 2, way).wait_recv()
            total = (
                xbuf[x, q].astype(f32) + x2[0, q].astype(f32) + x2[1, q].astype(f32)
            )
            zsum[q] = total.astype(bf16)
            for k in range(ZN - 1):
                z_copy(q, k).start()
        if q < C:
            for way in (0, 1):
                y_copy(q, 1, way).wait_recv()
                y_copy(q, 2, way).wait_recv()
            a, first = divmod(q * CW, D)

            def adam_step(i, carry, a=a, first=first, q=q):
                r = pl.ds(pl.multiple_of(i * 16, 16), 16)
                cols = pl.ds(first, CW)
                grad = (
                    gbuf[q, y, r, :].astype(f32)
                    + y2[0, q, r, :].astype(f32)
                    + y2[1, q, r, :].astype(f32)
                )
                if a == 0:
                    grad = grad * INV
                m = beta_one * state[2 * a, r, cols] + (1.0 - beta_one) * grad
                v = beta_two * state[2 * a + 1, r, cols] + (1.0 - beta_two) * grad * grad
                old = rows[a, pl.ds(pl.multiple_of(y * OWN + i * 16, 16), 16), cols]
                new = old.astype(f32) - learn_rate * m / (jnp.sqrt(v) + adam_eps)
                (down_ref if a == 0 else up_ref)[r, cols] = new.astype(bf16)
                return carry

            lax.fori_loop(0, OWN // 16, adam_step, 0)

    scale = jnp.where(c == 1, INV, 1.0).astype(f32)
    for q in range(Q):
        total = zsum[q, z].astype(f32)
        for k in range(ZN - 1):
            z_copy(q, k).wait_recv()
            total = total + zrecv[q, k].astype(f32)
        fin[q * R // 32, pl.ds(q * R % 32, R), :] = (total * scale).astype(bf16)
    send_fin = remote(fin.at[1 - c], fpeer, pair_send.at[2], pair_recv.at[2], sibling)
    send_fin.start()
    mine = fin[c]
    send_fin.wait_recv()
    peer = fpeer[...]
    layer_ref[...] = jnp.where(c == 0, mine, peer)
    input_ref[...] = jnp.where(c == 0, peer, mine)

    send_rows.wait_send()
    send_ws.wait_send()
    send_fin.wait_send()
    for kind in range(3):
        for way in (0, 1):
            for q in range(C):
                y_copy(q, kind, way).wait_send()
            for q in range(Q):
                x_copy(q, kind, way).wait_send()
    for q in range(Q):
        for k in range(ZN - 1):
            z_copy(q, k).wait_send()


def exchange(coef, rows, acts, dm, dv, um, uv):
    hbm = pl.BlockSpec(memory_space=pltpu.HBM)
    vmem = pl.BlockSpec(memory_space=pltpu.VMEM)
    dma = pltpu.SemaphoreType.DMA
    return pl.pallas_call(
        main_kernel,
        out_shape=(
            jax.ShapeDtypeStruct((32, T), bf16),
            jax.ShapeDtypeStruct((32, T), bf16),
            jax.ShapeDtypeStruct((OWN, D), bf16),
            jax.ShapeDtypeStruct((OWN, D), bf16),
        ),
        in_specs=[vmem] * 3 + [hbm] * 4,
        out_specs=(vmem,) * 4,
        scratch_shapes=[
            pltpu.VMEM((E, D), bf16),
            pltpu.VMEM((2, E, T), bf16),
            pltpu.VMEM((E, T), bf16),
            pltpu.VMEM((4, OWN, D), f32),
            pltpu.VMEM((C, YN, OWN, CW), bf16),
            pltpu.VMEM((2, C, OWN // 2, CW), bf16),
            pltpu.VMEM((2, C, OWN, CW), bf16),
            pltpu.VMEM((XN, Q, ZN, R, T), bf16),
            pltpu.VMEM((2, Q, ZN // 2, R, T), bf16),
            pltpu.VMEM((2, Q, ZN, R, T), bf16),
            pltpu.VMEM((Q, ZN, R, T), bf16),
            pltpu.VMEM((Q, ZN - 1, R, T), bf16),
            pltpu.VMEM((2, 32, T), bf16),
            pltpu.VMEM((32, T), bf16),
            dma((4,)),
            dma((3,)),
            dma((3,)),
            dma((3, 2, C)),
            dma((3, 2, C)),
            dma((3, 2, Q)),
            dma((3, 2, Q)),
            dma((Q, ZN - 1)),
            dma((Q, ZN - 1)),
        ],
        compiler_params=pltpu.CompilerParams(
            collective_id=0, has_side_effects=True, vmem_limit_bytes=36 * 1024 * 1024
        ),
    )(coef, rows, acts, dm, dv, um, uv)


def local(
    tokens, picks, route_weight, out_grad, down_rows, up_rows, down_mom, down_var, up_mom, up_var
):
    picks_t = picks.transpose(1, 2, 0).reshape(NP, T)
    weight_t = route_weight.transpose(1, 2, 0).reshape(NP, T)
    in_hbm = functools.partial(pltpu.with_memory_space_constraint, memory_space=pltpu.HBM)
    coef, rows, acts = coefficients(
        *map(in_hbm, (picks_t, weight_t, down_rows, tokens, up_rows, out_grad))
    )
    layer, grad, new_down, new_up = exchange(
        coef, rows, acts, *map(in_hbm, (down_mom, down_var, up_mom, up_var))
    )
    return (layer.T, grad.T, new_down, new_up)


def solution(mesh):
    placed = (
        P("dp", None),
        P("dp", None, None),
        P("dp", None, None),
        P("dp", None),
        P("expert", None),
        P("expert", None),
        P(("expert", "dp"), None),
        P(("expert", "dp"), None),
        P(("expert", "dp"), None),
        P(("expert", "dp"), None),
    )
    return jax.shard_map(
        local,
        mesh=mesh,
        in_specs=placed,
        out_specs=(
            P("dp", "expert"),
            P("dp", "expert"),
            P(("expert", "dp"), None),
            P(("expert", "dp"), None),
        ),
        check_vma=False,
    )
```

```python
import functools
import math

import jax
import jax.numpy as jnp
from jax import lax
from jax.experimental import pallas as pl
from jax.experimental.pallas import tpu as pltpu
from jax.sharding import PartitionSpec as P

gelu_root = 0.7978845608
gelu_cube = 0.044715
learn_rate = 0.05
beta_one = 0.9
beta_two = 0.999
adam_eps = 1e-08

D = 2048
E = 256
T = 512
NP = 128
OWN = 64
YN, XN, ZN = 4, 4, 8
Q = 2
R = 64 // Q
TA = 256
TB = T - TA
C = 4
CW = 2 * D // C
INV = 1.0 / math.sqrt(D)
MESH = pl.DeviceIdType.MESH
f32 = jnp.float32
bf16 = jnp.bfloat16


def coefficient_kernel(
    picks_hbm, weight_hbm, down_hbm, tok_hbm, up_hbm, cot_hbm,
    coef_ref, rows_ref, acts_ref, key_ref, weight_ref, sem,
):
    loads = []
    for i, (src, dst) in enumerate((
        (picks_hbm, key_ref), (weight_hbm, weight_ref),
        (down_hbm, rows_ref.at[0]), (tok_hbm, acts_ref.at[0]),
        (up_hbm, rows_ref.at[1]), (cot_hbm, acts_ref.at[1]),
    )):
        copy = pltpu.make_async_copy(src, dst, sem.at[i])
        copy.start()
        loads.append(copy)
    coef_ref[...] = jnp.zeros((E, T), f32)
    loads[0].wait()
    first = lax.axis_index("expert") * E
    key = key_ref[...] - first
    own = jnp.logical_and(key >= 0, key < E)
    key_ref[...] = jnp.where(own, key, -1)
    rounds = jnp.max(jnp.sum(own.astype(jnp.int32), axis=0, keepdims=True))
    loads[1].wait()

    def one_round(_, last):
        keys = key_ref[...]
        now = jnp.max(jnp.where(keys < last, keys, -1), axis=0, keepdims=True)
        total = jnp.sum(
            jnp.where(keys == now, weight_ref[...], 0.0), axis=0, keepdims=True
        )
        ids = lax.broadcasted_iota(jnp.int32, (E, T), 0)
        coef_ref[...] = jnp.where(ids == now, total, coef_ref[...])
        return now

    lax.fori_loop(0, rounds, one_round, jnp.full((1, T), E, jnp.int32))
    for copy in loads[2:]:
        copy.wait()


def coefficients(picks, weights, down_rows, tokens, up_rows, out_grad):
    vmem = pl.BlockSpec(memory_space=pltpu.VMEM)
    hbm = pl.BlockSpec(memory_space=pltpu.HBM)
    return pl.pallas_call(
        coefficient_kernel,
        out_shape=(
            pltpu.VMEM((E, T), f32),
            pltpu.VMEM((2, E, D), bf16),
            pltpu.VMEM((2, T, D), bf16),
        ),
        in_specs=[hbm] * 6,
        out_specs=(vmem, vmem, vmem),
        scratch_shapes=[
            pltpu.VMEM((NP, T), jnp.int32),
            pltpu.VMEM((NP, T), f32),
            pltpu.SemaphoreType.DMA((6,)),
        ],
        compiler_params=pltpu.CompilerParams(vmem_limit_bytes=24 * 1024 * 1024),
    )(picks, weights, down_rows, tokens, up_rows, out_grad)


def main_kernel(
    coef, rows, acts, dm_hbm, dv_hbm, um_hbm, uv_hbm,
    layer_ref, input_ref, down_ref, up_ref,
    prow, ws, pws, state,
    gbuf, y1, y2, xbuf, x1, x2, asum, arecv,
    zbuf, z1, z2, z3, z4, bsum, brecv, fin, fpeer,
    load_sem, pair_send, pair_recv, y_send, y_recv, x_send, x_recv,
    z_send, z_recv, a_send, a_recv, b_send, b_recv,
):
    y = lax.axis_index("dp")
    e = lax.axis_index("expert")
    c = lax.rem(e, 2)
    z = lax.rem(e // 2, ZN)
    x = e // (2 * ZN)

    def at(xx, zz):
        return (y, (xx * ZN + zz) * 2 + c)

    def xat(k):
        return lax.rem(x + k + XN, XN)

    def zat(k):
        return lax.rem(z + k + ZN, ZN)

    def yat(k):
        return lax.rem(y + k + YN, YN)

    sibling = (y, (x * ZN + z) * 2 + 1 - c)

    loads = []
    for i, (src, dst) in enumerate((
        (dm_hbm, state.at[0]), (dv_hbm, state.at[1]),
        (um_hbm, state.at[2]), (uv_hbm, state.at[3]),
    )):
        copy = pltpu.make_async_copy(src, dst, load_sem.at[i])
        copy.start()
        loads.append(copy)

    barrier = pltpu.get_barrier_semaphore()
    greet = [sibling, (yat(1), e), (yat(-1), e)]
    greet += [at(xat(k), z) for k in range(1, XN)]
    greet += [at(x, zat(k)) for k in range(1, ZN)]
    for who in greet:
        pl.semaphore_signal(barrier, inc=1, device_id=who, device_id_type=MESH)

    def remote(src, dst, send, recv, who):
        return pltpu.make_async_remote_copy(
            src_ref=src, dst_ref=dst, send_sem=send, recv_sem=recv,
            device_id=who, device_id_type=MESH,
        )

    def y_copy(q, kind, way):
        low = (kind != 1) == (way == 0)
        near = 1 if way == 0 else -1
        block = yat(2 if kind == 0 else near)
        half = pl.ds(0 if low else OWN // 2, OWN // 2)
        src = gbuf.at[q, block, half, :]
        dst = y1.at[way, q] if kind == 0 else y2.at[way, q, half, :]
        sems = y_send.at[kind, way, q], y_recv.at[kind, way, q]
        return remote(src, dst, *sems, (yat(near), e))

    def x_copy(q, kind, way):
        low = (kind != 1) == (way == 0)
        near = 1 if way == 0 else -1
        block = xat(2 if kind == 0 else near)
        half = pl.ds(0 if low else ZN // 2, ZN // 2)
        src = xbuf.at[block, q, half]
        dst = x1.at[way, q] if kind == 0 else x2.at[way, q, half]
        sems = x_send.at[kind, way, q], x_recv.at[kind, way, q]
        return remote(src, dst, *sems, at(xat(near), z))

    def z_copy(q, kind, way):
        low = (kind != 1) == (way == 0)
        near = 1 if way == 0 else -1
        block = zat((4, 3, 3, 2, 1)[kind] * near)
        half = pl.ds(0 if low else XN // 2, XN // 2)
        src = zbuf.at[block, q] if kind > 2 else zbuf.at[block, q, half]
        if kind == 0:
            dst = z1.at[way, q]
        elif kind < 3:
            dst = z2.at[way, q, half]
        else:
            dst = (z3 if kind == 3 else z4).at[way, q]
        sems = z_send.at[kind, way, q], z_recv.at[kind, way, q]
        return remote(src, dst, *sems, at(x, zat(near)))

    def a_copy(q, k):
        p = zat(k + 1)
        sems = a_send.at[q, k], a_recv.at[q, k]
        return remote(asum.at[q, p], arecv.at[q, k], *sems, at(x, p))

    def b_copy(q, k):
        p = xat(k + 1)
        sems = b_send.at[q, k], b_recv.at[q, k]
        return remote(bsum.at[q, p], brecv.at[q, k], *sems, at(p, z))

    s = lax.dot_general(
        rows[0], acts[0], (((1,), (1,)), ((), ())), preferred_element_type=f32
    ) * INV
    b = lax.dot_general(
        rows[1], acts[1], (((1,), (1,)), ((), ())), preferred_element_type=f32
    )
    k = coef[...]
    u = jnp.tanh(gelu_root * (s + gelu_cube * s * s * s))
    ws[1] = (k * (0.5 * s * (1.0 + u))).astype(bf16)
    slope = 0.5 * (1.0 + u) + 0.5 * s * (1.0 - u * u) * gelu_root * (
        1.0 + 3.0 * gelu_cube * s * s
    )
    ws[0] = (k * slope * b).astype(bf16)
    pl.semaphore_wait(barrier, len(greet))
    send_rows = remote(rows.at[c], prow, pair_send.at[0], pair_recv.at[0], sibling)
    send_rows.start()
    send_ws = remote(ws.at[c], pws, pair_send.at[1], pair_recv.at[1], sibling)
    send_ws.start()

    def gradients(q):
        a, first = divmod(q * CW, D)
        g = jnp.dot(ws[a], acts[a, :, first : first + CW], preferred_element_type=f32)
        gbuf[q] = g.astype(bf16).reshape(YN, OWN, CW)
        for kind in (0, 1):
            for way in (0, 1):
                y_copy(q, kind, way).start()

    def partial_rows(block, tokens):
        cols = pl.ds(pl.multiple_of(block * 512, 512), 512)
        part = lax.dot_general(
            rows[1 - c, :, cols], ws[1 - c, :, tokens], (((0,), (0,)), ((), ())),
            preferred_element_type=f32,
        ) + lax.dot_general(
            prow[:, cols], pws[:, tokens], (((0,), (0,)), ((), ())),
            preferred_element_type=f32,
        )
        return part.astype(bf16)

    a_tokens, b_tokens = slice(0, TA), slice(TA, T)

    gradients(0)
    send_rows.wait_recv()
    send_ws.wait_recv()
    for i in range(XN):
        part = partial_rows(i, b_tokens)
        for j in range(ZN):
            for q in range(Q):
                r = j * 64 + q * R
                zbuf[j, q, i] = part[r : r + R, :]
    for q in range(Q):
        for way in (0, 1):
            z_copy(q, 0, way).start()
    for q in range(Q):
        for way in (0, 1):
            z_copy(q, 1, way).start()
    for step in (2, 1, -1, 0):
        block = xat(step)
        part = partial_rows(block, a_tokens)
        for j in range(ZN):
            for q in range(Q):
                r = j * 64 + q * R
                xbuf[block, q, j] = part[r : r + R, :]
        for q in range(Q):
            if step == 2:
                x_copy(q, 0, 0).start()
                x_copy(q, 0, 1).start()
            elif step:
                x_copy(q, 1, 0 if step == 1 else 1).start()
        if step == 2:
            gradients(1)
    gradients(2)
    gradients(3)

    def z_relay(q, kind):
        for way in (0, 1):
            near = 1 if way == 0 else -1
            if kind == 0:
                z_copy(q, 0, way).wait_recv()
                block = zat(3 * near)
                half = pl.ds(0 if way == 0 else XN // 2, XN // 2)
                mine = zbuf[block, q, half].astype(f32)
                zbuf[block, q, half] = (mine + z1[way, q].astype(f32)).astype(bf16)
                z_copy(q, 2, way).start()
            else:
                if kind == 2:
                    z_copy(q, 1, way).wait_recv()
                z_copy(q, kind, way).wait_recv()
                block = zat((2 if kind == 2 else 1) * near)
                got = (z2 if kind == 2 else z3)[way, q].astype(f32)
                zbuf[block, q] = (zbuf[block, q].astype(f32) + got).astype(bf16)
                z_copy(q, kind + 1, way).start()

    def x_relay(q):
        for way in (0, 1):
            x_copy(q, 0, way).wait_recv()
            block = xat(1 if way == 0 else -1)
            half = pl.ds(0 if way == 0 else ZN // 2, ZN // 2)
            mine = xbuf[block, q, half].astype(f32)
            xbuf[block, q, half] = (mine + x1[way, q].astype(f32)).astype(bf16)
            x_copy(q, 2, way).start()

    def y_relay(q):
        for way in (0, 1):
            y_copy(q, 0, way).wait_recv()
            block = yat(1 if way == 0 else -1)
            half = pl.ds(0 if way == 0 else OWN // 2, OWN // 2)
            mine = gbuf[q, block, half, :].astype(f32)
            gbuf[q, block, half, :] = (mine + y1[way, q].astype(f32)).astype(bf16)
            y_copy(q, 2, way).start()

    def x_finish(q):
        for way in (0, 1):
            x_copy(q, 1, way).wait_recv()
            x_copy(q, 2, way).wait_recv()
        total = xbuf[x, q].astype(f32) + x2[0, q].astype(f32) + x2[1, q].astype(f32)
        asum[q] = total.astype(bf16)
        for k in (3, 2, 4, 1, 5, 0, 6):
            a_copy(q, k).start()

    def z_finish(q):
        for way in (0, 1):
            z_copy(q, 4, way).wait_recv()
        total = zbuf[z, q].astype(f32) + z4[0, q].astype(f32) + z4[1, q].astype(f32)
        bsum[q] = total.astype(bf16)
        for k in (1, 0, 2):
            b_copy(q, k).start()

    def adam(q):
        for way in (0, 1):
            y_copy(q, 1, way).wait_recv()
            y_copy(q, 2, way).wait_recv()
        a, first = divmod(q * CW, D)

        def adam_step(i, carry):
            r = pl.ds(pl.multiple_of(i * 16, 16), 16)
            cols = pl.ds(first, CW)
            grad = (
                gbuf[q, y, r, :].astype(f32)
                + y2[0, q, r, :].astype(f32)
                + y2[1, q, r, :].astype(f32)
            )
            if a == 0:
                grad = grad * INV
            m = beta_one * state[2 * a, r, cols] + (1.0 - beta_one) * grad
            v = beta_two * state[2 * a + 1, r, cols] + (1.0 - beta_two) * grad * grad
            old = rows[a, pl.ds(pl.multiple_of(y * OWN + i * 16, 16), 16), cols]
            new = old.astype(f32) - learn_rate * m / (jnp.sqrt(v) + adam_eps)
            (down_ref if a == 0 else up_ref)[r, cols] = new.astype(bf16)
            return carry

        lax.fori_loop(0, OWN // 16, adam_step, 0)

    scale = jnp.where(c == 1, INV, 1.0).astype(f32)

    def finish(q):
        place = q * R // 32, pl.ds(q * R % 32, R)
        total = bsum[q, x].astype(f32)
        for k in range(XN - 1):
            b_copy(q, k).wait_recv()
            total = total + brecv[q, k].astype(f32)
        fin[place[0], place[1], b_tokens] = (total * scale).astype(bf16)
        total = asum[q, z].astype(f32)
        for k in range(ZN - 1):
            a_copy(q, k).wait_recv()
            total = total + arecv[q, k].astype(f32)
        fin[place[0], place[1], a_tokens] = (total * scale).astype(bf16)

    every = range(Q)
    for q in every:
        z_relay(q, 0)
    for q in every:
        x_relay(q)
    y_relay(0)
    for q in every:
        z_relay(q, 2)
    y_relay(1)
    y_relay(2)
    y_relay(3)
    for q in every:
        z_relay(q, 3)
    for q in every:
        x_finish(q)
    for q in every:
        z_finish(q)
    for copy in loads:
        copy.wait()
    adam(0)
    adam(1)
    for q in every:
        finish(q)
    send_fin = remote(fin.at[1 - c], fpeer, pair_send.at[2], pair_recv.at[2], sibling)
    send_fin.start()
    adam(2)
    adam(3)
    mine = fin[c]
    send_fin.wait_recv()
    peer = fpeer[...]
    layer_ref[...] = jnp.where(c == 0, mine, peer)
    input_ref[...] = jnp.where(c == 0, peer, mine)

    send_rows.wait_send()
    send_ws.wait_send()
    send_fin.wait_send()
    for way in (0, 1):
        for q in range(C):
            for kind in range(3):
                y_copy(q, kind, way).wait_send()
        for q in range(Q):
            for kind in range(3):
                x_copy(q, kind, way).wait_send()
            for kind in range(5):
                z_copy(q, kind, way).wait_send()
    for q in range(Q):
        for k in range(ZN - 1):
            a_copy(q, k).wait_send()
        for k in range(XN - 1):
            b_copy(q, k).wait_send()


def exchange(coef, rows, acts, dm, dv, um, uv):
    hbm = pl.BlockSpec(memory_space=pltpu.HBM)
    vmem = pl.BlockSpec(memory_space=pltpu.VMEM)
    dma = pltpu.SemaphoreType.DMA
    return pl.pallas_call(
        main_kernel,
        out_shape=(
            pltpu.VMEM((32, T), bf16),
            pltpu.VMEM((32, T), bf16),
            pltpu.VMEM((OWN, D), bf16),
            pltpu.VMEM((OWN, D), bf16),
        ),
        in_specs=[vmem] * 3 + [hbm] * 4,
        out_specs=(vmem,) * 4,
        scratch_shapes=[
            pltpu.VMEM((E, D), bf16),
            pltpu.VMEM((2, E, T), bf16),
            pltpu.VMEM((E, T), bf16),
            pltpu.VMEM((4, OWN, D), f32),
            pltpu.VMEM((C, YN, OWN, CW), bf16),
            pltpu.VMEM((2, C, OWN // 2, CW), bf16),
            pltpu.VMEM((2, C, OWN, CW), bf16),
            pltpu.VMEM((XN, Q, ZN, R, TA), bf16),
            pltpu.VMEM((2, Q, ZN // 2, R, TA), bf16),
            pltpu.VMEM((2, Q, ZN, R, TA), bf16),
            pltpu.VMEM((Q, ZN, R, TA), bf16),
            pltpu.VMEM((Q, ZN - 1, R, TA), bf16),
            pltpu.VMEM((ZN, Q, XN, R, TB), bf16),
            pltpu.VMEM((2, Q, XN // 2, R, TB), bf16),
            pltpu.VMEM((2, Q, XN, R, TB), bf16),
            pltpu.VMEM((2, Q, XN, R, TB), bf16),
            pltpu.VMEM((2, Q, XN, R, TB), bf16),
            pltpu.VMEM((Q, XN, R, TB), bf16),
            pltpu.VMEM((Q, XN - 1, R, TB), bf16),
            pltpu.VMEM((2, 32, T), bf16),
            pltpu.VMEM((32, T), bf16),
            dma((4,)),
            dma((3,)),
            dma((3,)),
            dma((3, 2, C)),
            dma((3, 2, C)),
            dma((3, 2, Q)),
            dma((3, 2, Q)),
            dma((5, 2, Q)),
            dma((5, 2, Q)),
            dma((Q, ZN - 1)),
            dma((Q, ZN - 1)),
            dma((Q, XN - 1)),
            dma((Q, XN - 1)),
        ],
        compiler_params=pltpu.CompilerParams(
            collective_id=0, has_side_effects=True, vmem_limit_bytes=36 * 1024 * 1024
        ),
    )(coef, rows, acts, dm, dv, um, uv)


def write_kernel(*refs):
    copies = [pltpu.make_async_copy(refs[i], refs[4 + i], refs[8].at[i]) for i in range(4)]
    for copy in copies:
        copy.start()
    for copy in copies:
        copy.wait()


def write_out(*arrays):
    return pl.pallas_call(
        write_kernel,
        out_shape=tuple(jax.ShapeDtypeStruct(a.shape, a.dtype) for a in arrays),
        in_specs=[pl.BlockSpec(memory_space=pltpu.VMEM)] * 4,
        out_specs=(pl.BlockSpec(memory_space=pltpu.HBM),) * 4,
        scratch_shapes=[pltpu.SemaphoreType.DMA((4,))],
        compiler_params=pltpu.CompilerParams(vmem_limit_bytes=4 * 1024 * 1024),
    )(*(pltpu.with_memory_space_constraint(a, pltpu.VMEM) for a in arrays))


def local(
    tokens, picks, route_weight, out_grad, down_rows, up_rows, down_mom, down_var, up_mom, up_var
):
    picks_t = picks.transpose(1, 2, 0).reshape(NP, T)
    weight_t = route_weight.transpose(1, 2, 0).reshape(NP, T)
    in_hbm = functools.partial(pltpu.with_memory_space_constraint, memory_space=pltpu.HBM)
    coef, rows, acts = coefficients(
        *map(in_hbm, (picks_t, weight_t, down_rows, tokens, up_rows, out_grad))
    )
    layer, grad, new_down, new_up = write_out(*exchange(
        coef, rows, acts, *map(in_hbm, (down_mom, down_var, up_mom, up_var))
    ))
    return (layer.T, grad.T, new_down, new_up)


def solution(mesh):
    placed = (
        P("dp", None),
        P("dp", None, None),
        P("dp", None, None),
        P("dp", None),
        P("expert", None),
        P("expert", None),
        P(("expert", "dp"), None),
        P(("expert", "dp"), None),
        P(("expert", "dp"), None),
        P(("expert", "dp"), None),
    )
    return jax.shard_map(
        local,
        mesh=mesh,
        in_specs=placed,
        out_specs=(
            P("dp", "expert"),
            P("dp", "expert"),
            P(("expert", "dp"), None),
            P(("expert", "dp"), None),
        ),
        check_vma=False,
    )
```

```python
import functools
import math

import jax
import jax.numpy as jnp
from jax import lax
from jax.experimental import pallas as pl
from jax.experimental.pallas import tpu as pltpu
from jax.sharding import PartitionSpec as P

gelu_root = 0.7978845608
gelu_cube = 0.044715
learn_rate = 0.05
beta_one = 0.9
beta_two = 0.999
adam_eps = 1e-08

D = 2048
E = 256
T = 512
NP = 128
OWN = 64
YN, XN, ZN = 4, 4, 8
Q = 2
R = 64 // Q
TA = 256
TB = T - TA
C = 4
CW = 2 * D // C
INV = 1.0 / math.sqrt(D)
MESH = pl.DeviceIdType.MESH
f32 = jnp.float32
bf16 = jnp.bfloat16


def coefficient_kernel(
    picks_hbm, weight_hbm, down_hbm, tok_hbm, up_hbm, cot_hbm,
    coef_ref, rows_ref, acts_ref, key_ref, weight_ref, sem,
):
    loads = []
    for i, (src, dst) in enumerate((
        (picks_hbm, key_ref), (weight_hbm, weight_ref),
        (down_hbm, rows_ref.at[0]), (tok_hbm, acts_ref.at[0]),
        (up_hbm, rows_ref.at[1]), (cot_hbm, acts_ref.at[1]),
    )):
        copy = pltpu.make_async_copy(src, dst, sem.at[i])
        copy.start()
        loads.append(copy)
    coef_ref[...] = jnp.zeros((E, T), f32)
    loads[0].wait()
    first = lax.axis_index("expert") * E
    key = key_ref[...] - first
    own = jnp.logical_and(key >= 0, key < E)
    key_ref[...] = jnp.where(own, key, -1)
    rounds = jnp.max(jnp.sum(own.astype(jnp.int32), axis=0, keepdims=True))
    loads[1].wait()

    def one_round(_, last):
        keys = key_ref[...]
        now = jnp.max(jnp.where(keys < last, keys, -1), axis=0, keepdims=True)
        total = jnp.sum(
            jnp.where(keys == now, weight_ref[...], 0.0), axis=0, keepdims=True
        )
        ids = lax.broadcasted_iota(jnp.int32, (E, T), 0)
        coef_ref[...] = jnp.where(ids == now, total, coef_ref[...])
        return now

    lax.fori_loop(0, rounds, one_round, jnp.full((1, T), E, jnp.int32))
    for copy in loads[2:]:
        copy.wait()


def coefficients(picks, weights, down_rows, tokens, up_rows, out_grad):
    vmem = pl.BlockSpec(memory_space=pltpu.VMEM)
    hbm = pl.BlockSpec(memory_space=pltpu.HBM)
    return pl.pallas_call(
        coefficient_kernel,
        out_shape=(
            pltpu.VMEM((E, T), f32),
            pltpu.VMEM((2, E, D), bf16),
            pltpu.VMEM((2, T, D), bf16),
        ),
        in_specs=[hbm] * 6,
        out_specs=(vmem, vmem, vmem),
        scratch_shapes=[
            pltpu.VMEM((NP, T), jnp.int32),
            pltpu.VMEM((NP, T), f32),
            pltpu.SemaphoreType.DMA((6,)),
        ],
        compiler_params=pltpu.CompilerParams(vmem_limit_bytes=24 * 1024 * 1024),
    )(picks, weights, down_rows, tokens, up_rows, out_grad)


def main_kernel(
    coef, rows, acts, dm_hbm, dv_hbm, um_hbm, uv_hbm,
    layer_ref, input_ref, down_ref, up_ref,
    prow, ws, pws, state,
    gbuf, y1, y2, xbuf, x2, asum, arecv,
    zbuf, z1, z2, z3, z4, bsum, brecv, fin, fpeer,
    load_sem, pair_send, pair_recv, y_send, y_recv, x_send, x_recv,
    z_send, z_recv, a_send, a_recv, b_send, b_recv,
):
    y = lax.axis_index("dp")
    e = lax.axis_index("expert")
    c = lax.rem(e, 2)
    z = lax.rem(e // 2, ZN)
    x = e // (2 * ZN)

    def at(xx, zz, cc=c):
        return (y, (xx * ZN + zz) * 2 + cc)

    def xat(k):
        return lax.rem(x + k + XN, XN)

    def zat(k):
        return lax.rem(z + k + ZN, ZN)

    def yat(k):
        return lax.rem(y + k + YN, YN)

    sibling = (y, (x * ZN + z) * 2 + 1 - c)

    loads = []
    for i, (src, dst) in enumerate((
        (dm_hbm, state.at[0]), (dv_hbm, state.at[1]),
        (um_hbm, state.at[2]), (uv_hbm, state.at[3]),
    )):
        copy = pltpu.make_async_copy(src, dst, load_sem.at[i])
        copy.start()
        loads.append(copy)

    barrier = pltpu.get_barrier_semaphore()
    greet = [sibling, (yat(1), e), (yat(-1), e)]
    for cc in (c,):
        greet += [at(xat(k), z, cc) for k in range(1, XN)]
        greet += [at(x, zat(k), cc) for k in range(1, ZN)]
    for who in greet:
        pl.semaphore_signal(barrier, inc=1, device_id=who, device_id_type=MESH)

    def remote(src, dst, send, recv, who):
        return pltpu.make_async_remote_copy(
            src_ref=src, dst_ref=dst, send_sem=send, recv_sem=recv,
            device_id=who, device_id_type=MESH,
        )

    def y_copy(q, kind, way):
        low = (kind != 1) == (way == 0)
        near = 1 if way == 0 else -1
        block = yat(2 if kind == 0 else near)
        half = pl.ds(0 if low else OWN // 2, OWN // 2)
        src = gbuf.at[q, block, half, :]
        dst = y1.at[way, q] if kind == 0 else y2.at[way, q, half, :]
        sems = y_send.at[kind, way, q], y_recv.at[kind, way, q]
        return remote(src, dst, *sems, (yat(near), e))

    def x_copy(q, k):
        p = xat(k + 1)
        sems = x_send.at[q, k], x_recv.at[q, k]
        return remote(xbuf.at[p, q], x2.at[k, q], *sems, at(p, z))

    def z_copy(q, kind, way):
        low = (kind != 1) == (way == 0)
        near = 1 if way == 0 else -1
        block = zat((4, 3, 3, 2, 1)[kind] * near)
        half = pl.ds(0 if low else XN // 2, XN // 2)
        src = zbuf.at[block, q] if kind > 2 else zbuf.at[block, q, half]
        if kind == 0:
            dst = z1.at[way, q]
        elif kind < 3:
            dst = z2.at[way, q, half]
        else:
            dst = (z3 if kind == 3 else z4).at[way, q]
        sems = z_send.at[kind, way, q], z_recv.at[kind, way, q]
        return remote(src, dst, *sems, at(x, zat(near)))

    def a_copy(q, k):
        p = zat(k + 1)
        sems = a_send.at[q, k], a_recv.at[q, k]
        return remote(asum.at[q, p], arecv.at[q, k], *sems, at(x, p))

    def b_copy(q, k):
        p = xat(k + 1)
        sems = b_send.at[q, k], b_recv.at[q, k]
        return remote(bsum.at[q, p], brecv.at[q, k], *sems, at(p, z))

    def pair_copy(i, src, dst):
        return remote(src, dst, pair_send.at[i], pair_recv.at[i], sibling)

    send_rows = pair_copy(0, rows.at[c], prow)
    send_ws = pair_copy(1, ws.at[c], pws)
    send_fin = pair_copy(2, fin.at[1 - c], fpeer)

    s = lax.dot_general(
        rows[0], acts[0], (((1,), (1,)), ((), ())), preferred_element_type=f32
    ) * INV
    pl.semaphore_wait(barrier, len(greet))
    send_rows.start()
    b = lax.dot_general(
        rows[1], acts[1], (((1,), (1,)), ((), ())), preferred_element_type=f32
    )
    k = coef[...]
    u = jnp.tanh(gelu_root * (s + gelu_cube * s * s * s))
    ws[1] = (k * (0.5 * s * (1.0 + u))).astype(bf16)
    slope = 0.5 * (1.0 + u) + 0.5 * s * (1.0 - u * u) * gelu_root * (
        1.0 + 3.0 * gelu_cube * s * s
    )
    ws[0] = (k * slope * b).astype(bf16)
    send_ws.start()

    def gradients(q):
        a, first = divmod(q * CW, D)
        g = jnp.dot(ws[a], acts[a, :, first : first + CW], preferred_element_type=f32)
        gbuf[q] = g.astype(bf16).reshape(YN, OWN, CW)
        for kind in (0, 1) if q == 0 else (0,):
            for way in (0, 1):
                y_copy(q, kind, way).start()

    def partial_rows(block, tokens):
        cols = pl.ds(pl.multiple_of(block * 512, 512), 512)
        part = lax.dot_general(
            rows[1 - c, :, cols], ws[1 - c, :, tokens], (((0,), (0,)), ((), ())),
            preferred_element_type=f32,
        ) + lax.dot_general(
            prow[:, cols], pws[:, tokens], (((0,), (0,)), ((), ())),
            preferred_element_type=f32,
        )
        return part.astype(bf16)

    a_tokens, b_tokens = slice(0, TA), slice(TA, T)

    gradients(0)
    send_rows.wait_recv()
    send_ws.wait_recv()
    for i in range(XN):
        part = partial_rows(i, b_tokens)
        for j in range(ZN):
            for q in range(Q):
                r = j * 64 + q * R
                zbuf[j, q, i] = part[r : r + R, :]
    for q in range(Q):
        for way in (0, 1):
            z_copy(q, 0, way).start()
    for way in (0, 1):
        z_copy(0, 1, way).start()
    for step in (2, 1, -1, 0):
        block = xat(step)
        part = partial_rows(block, a_tokens)
        for j in range(ZN):
            for q in range(Q):
                r = j * 64 + q * R
                xbuf[block, q, j] = part[r : r + R, :]
        if step:
            x_copy(0, step - 1 if step > 0 else 2).start()
        if step == -1:
            for k in (1, 0, 2):
                x_copy(1, k).start()
            gradients(1)
    gradients(2)
    gradients(3)
    for way in (0, 1):
        y_copy(1, 1, way).start()

    def z_relay(q, kind):
        for way in (0, 1):
            near = 1 if way == 0 else -1
            if kind == 0:
                z_copy(q, 0, way).wait_recv()
                block = zat(3 * near)
                half = pl.ds(0 if way == 0 else XN // 2, XN // 2)
                mine = zbuf[block, q, half].astype(f32)
                zbuf[block, q, half] = (mine + z1[way, q].astype(f32)).astype(bf16)
                z_copy(q, 2, way).start()
                if q + 1 < Q:
                    z_copy(q + 1, 1, way).start()
            else:
                if kind == 2:
                    z_copy(q, 1, way).wait_recv()
                z_copy(q, kind, way).wait_recv()
                block = zat((2 if kind == 2 else 1) * near)
                got = (z2 if kind == 2 else z3)[way, q].astype(f32)
                zbuf[block, q] = (zbuf[block, q].astype(f32) + got).astype(bf16)
                z_copy(q, kind + 1, way).start()

    def y_relay(q):
        for way in (0, 1):
            y_copy(q, 0, way).wait_recv()
            block = yat(1 if way == 0 else -1)
            half = pl.ds(0 if way == 0 else OWN // 2, OWN // 2)
            mine = gbuf[q, block, half, :].astype(f32)
            gbuf[q, block, half, :] = (mine + y1[way, q].astype(f32)).astype(bf16)
            y_copy(q, 2, way).start()
            if q + 2 < C:
                y_copy(q + 2, 1, way).start()

    def x_finish(q):
        total = xbuf[x, q].astype(f32)
        for k in (2, 0, 1):
            x_copy(q, k).wait_recv()
            total = total + x2[k, q].astype(f32)
        asum[q] = total.astype(bf16)
        for k in (3, 2, 4, 1, 5, 0, 6):
            a_copy(q, k).start()

    def z_finish(q):
        for way in (0, 1):
            z_copy(q, 4, way).wait_recv()
        total = zbuf[z, q].astype(f32) + z4[0, q].astype(f32) + z4[1, q].astype(f32)
        bsum[q] = total.astype(bf16)
        for k in (1, 0, 2):
            b_copy(q, k).start()

    def adam(q):
        for way in (0, 1):
            y_copy(q, 1, way).wait_recv()
            y_copy(q, 2, way).wait_recv()
        a, first = divmod(q * CW, D)

        def adam_step(i, carry):
            r = pl.ds(pl.multiple_of(i * 16, 16), 16)
            cols = pl.ds(first, CW)
            grad = (
                gbuf[q, y, r, :].astype(f32)
                + y2[0, q, r, :].astype(f32)
                + y2[1, q, r, :].astype(f32)
            )
            if a == 0:
                grad = grad * INV
            m = beta_one * state[2 * a, r, cols] + (1.0 - beta_one) * grad
            v = beta_two * state[2 * a + 1, r, cols] + (1.0 - beta_two) * grad * grad
            old = rows[a, pl.ds(pl.multiple_of(y * OWN + i * 16, 16), 16), cols]
            new = old.astype(f32) - learn_rate * m / (jnp.sqrt(v) + adam_eps)
            (down_ref if a == 0 else up_ref)[r, cols] = new.astype(bf16)
            return carry

        lax.fori_loop(0, OWN // 16, adam_step, 0)

    scale = jnp.where(c == 1, INV, 1.0).astype(f32)

    def finish(q):
        total = asum[q, z].astype(f32)
        for k in range(ZN - 1):
            a_copy(q, k).wait_recv()
            total = total + arecv[q, k].astype(f32)
        fin[q, :, a_tokens] = (total * scale).astype(bf16)
        total = bsum[q, x].astype(f32)
        for k in range(XN - 1):
            b_copy(q, k).wait_recv()
            total = total + brecv[q, k].astype(f32)
        fin[q, :, b_tokens] = (total * scale).astype(bf16)

    z_relay(0, 0)
    z_relay(1, 0)
    z_relay(0, 2)
    z_relay(1, 2)
    y_relay(0)
    y_relay(1)
    z_relay(0, 3)
    z_relay(1, 3)
    x_finish(0)
    y_relay(2)
    y_relay(3)
    x_finish(1)
    z_finish(0)
    z_finish(1)
    for copy in loads:
        copy.wait()
    adam(0)
    adam(1)
    adam(2)
    finish(0)
    finish(1)
    send_fin.start()
    adam(3)
    mine = fin[c]
    send_fin.wait_recv()
    peer = fpeer[...]
    layer_ref[...] = jnp.where(c == 0, mine, peer)
    input_ref[...] = jnp.where(c == 0, peer, mine)

    send_rows.wait_send()
    send_ws.wait_send()
    send_fin.wait_send()
    for way in (0, 1):
        for q in range(C):
            for kind in range(3):
                y_copy(q, kind, way).wait_send()
        for q in range(Q):
            for kind in range(5):
                z_copy(q, kind, way).wait_send()
    for q in range(Q):
        for k in range(ZN - 1):
            a_copy(q, k).wait_send()
        for k in range(XN - 1):
            x_copy(q, k).wait_send()
            b_copy(q, k).wait_send()


def exchange(coef, rows, acts, dm, dv, um, uv):
    hbm = pl.BlockSpec(memory_space=pltpu.HBM)
    vmem = pl.BlockSpec(memory_space=pltpu.VMEM)
    dma = pltpu.SemaphoreType.DMA
    return pl.pallas_call(
        main_kernel,
        out_shape=(
            pltpu.VMEM((32, T), bf16),
            pltpu.VMEM((32, T), bf16),
            pltpu.VMEM((OWN, D), bf16),
            pltpu.VMEM((OWN, D), bf16),
        ),
        in_specs=[vmem] * 3 + [hbm] * 4,
        out_specs=(vmem,) * 4,
        scratch_shapes=[
            pltpu.VMEM((E, D), bf16),
            pltpu.VMEM((2, E, T), bf16),
            pltpu.VMEM((E, T), bf16),
            pltpu.VMEM((4, OWN, D), f32),
            pltpu.VMEM((C, YN, OWN, CW), bf16),
            pltpu.VMEM((2, C, OWN // 2, CW), bf16),
            pltpu.VMEM((2, C, OWN, CW), bf16),
            pltpu.VMEM((XN, Q, ZN, R, TA), bf16),
            pltpu.VMEM((XN - 1, Q, ZN, R, TA), bf16),
            pltpu.VMEM((Q, ZN, R, TA), bf16),
            pltpu.VMEM((2, ZN - 1, R, TA), bf16),
            pltpu.VMEM((ZN, Q, XN, R, TB), bf16),
            pltpu.VMEM((2, Q, XN // 2, R, TB), bf16),
            pltpu.VMEM((2, Q, XN, R, TB), bf16),
            pltpu.VMEM((2, Q, XN, R, TB), bf16),
            pltpu.VMEM((2, Q, XN, R, TB), bf16),
            pltpu.VMEM((Q, XN, R, TB), bf16),
            pltpu.VMEM((2, XN - 1, R, TB), bf16),
            pltpu.VMEM((2, 32, T), bf16),
            pltpu.VMEM((32, T), bf16),
            dma((4,)),
            dma((4,)),
            dma((4,)),
            dma((3, 2, C)),
            dma((3, 2, C)),
            dma((Q, XN - 1)),
            dma((Q, XN - 1)),
            dma((5, 2, Q)),
            dma((5, 2, Q)),
            dma((Q, ZN - 1)),
            dma((Q, ZN - 1)),
            dma((Q, XN - 1)),
            dma((Q, XN - 1)),
        ],
        compiler_params=pltpu.CompilerParams(
            collective_id=0, has_side_effects=True, vmem_limit_bytes=36 * 1024 * 1024
        ),
    )(coef, rows, acts, dm, dv, um, uv)


def write_kernel(*refs):
    copies = [pltpu.make_async_copy(refs[i], refs[4 + i], refs[8].at[i]) for i in range(4)]
    for copy in copies:
        copy.start()
    for copy in copies:
        copy.wait()


def write_out(*arrays):
    return pl.pallas_call(
        write_kernel,
        out_shape=tuple(jax.ShapeDtypeStruct(a.shape, a.dtype) for a in arrays),
        in_specs=[pl.BlockSpec(memory_space=pltpu.VMEM)] * 4,
        out_specs=(pl.BlockSpec(memory_space=pltpu.HBM),) * 4,
        scratch_shapes=[pltpu.SemaphoreType.DMA((4,))],
        compiler_params=pltpu.CompilerParams(vmem_limit_bytes=4 * 1024 * 1024),
    )(*(pltpu.with_memory_space_constraint(a, pltpu.VMEM) for a in arrays))


def local(
    tokens, picks, route_weight, out_grad, down_rows, up_rows, down_mom, down_var, up_mom, up_var
):
    picks_t = picks.transpose(1, 2, 0).reshape(NP, T)
    weight_t = route_weight.transpose(1, 2, 0).reshape(NP, T)
    in_hbm = functools.partial(pltpu.with_memory_space_constraint, memory_space=pltpu.HBM)
    coef, rows, acts = coefficients(
        *map(in_hbm, (picks_t, weight_t, down_rows, tokens, up_rows, out_grad))
    )
    layer, grad, new_down, new_up = write_out(*exchange(
        coef, rows, acts, *map(in_hbm, (down_mom, down_var, up_mom, up_var))
    ))
    return (layer.T, grad.T, new_down, new_up)


def solution(mesh):
    placed = (
        P("dp", None),
        P("dp", None, None),
        P("dp", None, None),
        P("dp", None),
        P("expert", None),
        P("expert", None),
        P(("expert", "dp"), None),
        P(("expert", "dp"), None),
        P(("expert", "dp"), None),
        P(("expert", "dp"), None),
    )
    return jax.shard_map(
        local,
        mesh=mesh,
        in_specs=placed,
        out_specs=(
            P("dp", "expert"),
            P("dp", "expert"),
            P(("expert", "dp"), None),
            P(("expert", "dp"), None),
        ),
        check_vma=False,
    )
```

```python
import functools
import math

import jax
import jax.numpy as jnp
from jax import lax
from jax.experimental import pallas as pl
from jax.experimental.pallas import tpu as pltpu
from jax.sharding import PartitionSpec as P

gelu_root = 0.7978845608
gelu_cube = 0.044715
learn_rate = 0.05
beta_one = 0.9
beta_two = 0.999
adam_eps = 1e-08

D = 2048
E = 256
T = 512
NP = 128
OWN = 64
YN, XN, ZN = 4, 4, 8
Q = 2
R = 64 // Q
TA = 256
TB = T - TA
C = 4
CW = 2 * D // C
INV = 1.0 / math.sqrt(D)
MESH = pl.DeviceIdType.MESH
f32 = jnp.float32
bf16 = jnp.bfloat16


def coefficient_kernel(
    picks_hbm, weight_hbm, down_hbm, tok_hbm, up_hbm,
    coef_ref, rows_ref, acts_ref, key_ref, weight_ref, sem,
):
    loads = []
    for i, (src, dst) in enumerate((
        (picks_hbm, key_ref), (weight_hbm, weight_ref),
        (down_hbm, rows_ref.at[0]), (tok_hbm, acts_ref),
        (up_hbm, rows_ref.at[1]),
    )):
        copy = pltpu.make_async_copy(src, dst, sem.at[i])
        copy.start()
        loads.append(copy)
    coef_ref[...] = jnp.zeros((E, T), f32)
    loads[0].wait()
    first = lax.axis_index("expert") * E
    key = key_ref[...] - first
    own = jnp.logical_and(key >= 0, key < E)
    key_ref[...] = jnp.where(own, key, -1)
    rounds = jnp.max(jnp.sum(own.astype(jnp.int32), axis=0, keepdims=True))
    loads[1].wait()

    def one_round(_, last):
        keys = key_ref[...]
        now = jnp.max(jnp.where(keys < last, keys, -1), axis=0, keepdims=True)
        total = jnp.sum(
            jnp.where(keys == now, weight_ref[...], 0.0), axis=0, keepdims=True
        )
        ids = lax.broadcasted_iota(jnp.int32, (E, T), 0)
        coef_ref[...] = jnp.where(ids == now, total, coef_ref[...])
        return now

    lax.fori_loop(0, rounds, one_round, jnp.full((1, T), E, jnp.int32))
    for copy in loads[2:]:
        copy.wait()


def coefficients(picks, weights, down_rows, tokens, up_rows):
    vmem = pl.BlockSpec(memory_space=pltpu.VMEM)
    hbm = pl.BlockSpec(memory_space=pltpu.HBM)
    return pl.pallas_call(
        coefficient_kernel,
        out_shape=(
            pltpu.VMEM((E, T), f32),
            pltpu.VMEM((2, E, D), bf16),
            pltpu.VMEM((T, D), bf16),
        ),
        in_specs=[hbm] * 5,
        out_specs=(vmem, vmem, vmem),
        scratch_shapes=[
            pltpu.VMEM((NP, T), jnp.int32),
            pltpu.VMEM((NP, T), f32),
            pltpu.SemaphoreType.DMA((5,)),
        ],
        compiler_params=pltpu.CompilerParams(vmem_limit_bytes=24 * 1024 * 1024),
    )(picks, weights, down_rows, tokens, up_rows)


def main_kernel(
    coef, rows, tok, cot_hbm, dm_hbm, dv_hbm, um_hbm, uv_hbm,
    layer_ref, input_ref, down_ref, up_ref,
    cot, prow, ws, pws, state,
    gbuf, y1, y2, xbuf, x2, asum, arecv,
    zbuf, z1, z2, z3, z4, bsum, brecv, fin, fpeer,
    load_sem, pair_send, pair_recv, y_send, y_recv, x_send, x_recv,
    z_send, z_recv, a_send, a_recv, b_send, b_recv,
):
    y = lax.axis_index("dp")
    e = lax.axis_index("expert")
    c = lax.rem(e, 2)
    z = lax.rem(e // 2, ZN)
    x = e // (2 * ZN)

    def at(xx, zz, cc=c):
        return (y, (xx * ZN + zz) * 2 + cc)

    def xat(k):
        return lax.rem(x + k + XN, XN)

    def zat(k):
        return lax.rem(z + k + ZN, ZN)

    def yat(k):
        return lax.rem(y + k + YN, YN)

    sibling = (y, (x * ZN + z) * 2 + 1 - c)

    loads = []
    for i, (src, dst) in enumerate((
        (cot_hbm, cot), (dm_hbm, state.at[0]), (dv_hbm, state.at[1]),
        (um_hbm, state.at[2]), (uv_hbm, state.at[3]),
    )):
        copy = pltpu.make_async_copy(src, dst, load_sem.at[i])
        copy.start()
        loads.append(copy)

    barrier = pltpu.get_barrier_semaphore()
    greet = [sibling, (yat(1), e), (yat(-1), e)]
    for cc in (c,):
        greet += [at(xat(k), z, cc) for k in range(1, XN)]
        greet += [at(x, zat(k), cc) for k in range(1, ZN)]
    for who in greet:
        pl.semaphore_signal(barrier, inc=1, device_id=who, device_id_type=MESH)

    def remote(src, dst, send, recv, who):
        return pltpu.make_async_remote_copy(
            src_ref=src, dst_ref=dst, send_sem=send, recv_sem=recv,
            device_id=who, device_id_type=MESH,
        )

    def y_copy(q, kind, way):
        low = (kind != 1) == (way == 0)
        near = 1 if way == 0 else -1
        block = yat(2 if kind == 0 else near)
        half = pl.ds(0 if low else OWN // 2, OWN // 2)
        src = gbuf.at[q, block, half, :]
        dst = y1.at[way, q] if kind == 0 else y2.at[way, q, half, :]
        sems = y_send.at[kind, way, q], y_recv.at[kind, way, q]
        return remote(src, dst, *sems, (yat(near), e))

    def x_copy(q, k):
        p = xat(k + 1)
        sems = x_send.at[q, k], x_recv.at[q, k]
        return remote(xbuf.at[p, q], x2.at[k, q], *sems, at(p, z))

    def z_copy(q, kind, way):
        low = (kind != 1) == (way == 0)
        near = 1 if way == 0 else -1
        block = zat((4, 3, 3, 2, 1)[kind] * near)
        half = pl.ds(0 if low else XN // 2, XN // 2)
        src = zbuf.at[block, q] if kind > 2 else zbuf.at[block, q, half]
        if kind == 0:
            dst = z1.at[way, q]
        elif kind < 3:
            dst = z2.at[way, q, half]
        else:
            dst = (z3 if kind == 3 else z4).at[way, q]
        sems = z_send.at[kind, way, q], z_recv.at[kind, way, q]
        return remote(src, dst, *sems, at(x, zat(near)))

    def a_copy(q, k):
        p = zat(k + 1)
        sems = a_send.at[q, k], a_recv.at[q, k]
        return remote(asum.at[q, p], arecv.at[q, k], *sems, at(x, p))

    def b_copy(q, k):
        p = xat(k + 1)
        sems = b_send.at[q, k], b_recv.at[q, k]
        return remote(bsum.at[q, p], brecv.at[q, k], *sems, at(p, z))

    def pair_copy(i, src, dst):
        return remote(src, dst, pair_send.at[i], pair_recv.at[i], sibling)

    send_rows = pair_copy(0, rows.at[c], prow)
    send_ws = pair_copy(1, ws.at[c], pws)
    send_fin = pair_copy(2, fin.at[1 - c], fpeer)

    s = lax.dot_general(
        rows[0], tok[...], (((1,), (1,)), ((), ())), preferred_element_type=f32
    ) * INV
    pl.semaphore_wait(barrier, len(greet))
    send_rows.start()
    loads[0].wait()
    b = lax.dot_general(
        rows[1], cot[...], (((1,), (1,)), ((), ())), preferred_element_type=f32
    )
    k = coef[...]
    u = jnp.tanh(gelu_root * (s + gelu_cube * s * s * s))
    ws[1] = (k * (0.5 * s * (1.0 + u))).astype(bf16)
    slope = 0.5 * (1.0 + u) + 0.5 * s * (1.0 - u * u) * gelu_root * (
        1.0 + 3.0 * gelu_cube * s * s
    )
    ws[0] = (k * slope * b).astype(bf16)
    send_ws.start()

    def gradients(q):
        a, first = divmod(q * CW, D)
        g = jnp.dot(
            ws[a], (tok, cot)[a][:, first : first + CW], preferred_element_type=f32
        )
        gbuf[q] = g.astype(bf16).reshape(YN, OWN, CW)
        for kind in (0, 1) if q == 0 else (0,):
            for way in (0, 1):
                y_copy(q, kind, way).start()

    def partial_rows(block, tokens):
        cols = pl.ds(pl.multiple_of(block * 512, 512), 512)
        part = lax.dot_general(
            rows[1 - c, :, cols], ws[1 - c, :, tokens], (((0,), (0,)), ((), ())),
            preferred_element_type=f32,
        ) + lax.dot_general(
            prow[:, cols], pws[:, tokens], (((0,), (0,)), ((), ())),
            preferred_element_type=f32,
        )
        return part.astype(bf16)

    a_tokens, b_tokens = slice(0, TA), slice(TA, T)

    gradients(0)
    send_rows.wait_recv()
    send_ws.wait_recv()
    for i in range(XN):
        part = partial_rows(i, b_tokens)
        for j in range(ZN):
            for q in range(Q):
                r = j * 64 + q * R
                zbuf[j, q, i] = part[r : r + R, :]
    for q in range(Q):
        for way in (0, 1):
            z_copy(q, 0, way).start()
    for way in (0, 1):
        z_copy(0, 1, way).start()
    for step in (2, 1, -1, 0):
        block = xat(step)
        part = partial_rows(block, a_tokens)
        for j in range(ZN):
            for q in range(Q):
                r = j * 64 + q * R
                xbuf[block, q, j] = part[r : r + R, :]
        if step:
            x_copy(0, step - 1 if step > 0 else 2).start()
        if step == -1:
            for k in (1, 0, 2):
                x_copy(1, k).start()
            gradients(1)
    gradients(2)
    gradients(3)
    for way in (0, 1):
        y_copy(1, 1, way).start()

    def z_relay(q, kind):
        for way in (0, 1):
            near = 1 if way == 0 else -1
            if kind == 0:
                z_copy(q, 0, way).wait_recv()
                block = zat(3 * near)
                half = pl.ds(0 if way == 0 else XN // 2, XN // 2)
                mine = zbuf[block, q, half].astype(f32)
                zbuf[block, q, half] = (mine + z1[way, q].astype(f32)).astype(bf16)
                z_copy(q, 2, way).start()
                if q + 1 < Q:
                    z_copy(q + 1, 1, way).start()
            else:
                if kind == 2:
                    z_copy(q, 1, way).wait_recv()
                z_copy(q, kind, way).wait_recv()
                block = zat((2 if kind == 2 else 1) * near)
                got = (z2 if kind == 2 else z3)[way, q].astype(f32)
                zbuf[block, q] = (zbuf[block, q].astype(f32) + got).astype(bf16)
                z_copy(q, kind + 1, way).start()

    def y_relay(q):
        for way in (0, 1):
            y_copy(q, 0, way).wait_recv()
            block = yat(1 if way == 0 else -1)
            half = pl.ds(0 if way == 0 else OWN // 2, OWN // 2)
            mine = gbuf[q, block, half, :].astype(f32)
            gbuf[q, block, half, :] = (mine + y1[way, q].astype(f32)).astype(bf16)
            y_copy(q, 2, way).start()
            if q + 2 < C:
                y_copy(q + 2, 1, way).start()

    def x_finish(q):
        total = xbuf[x, q].astype(f32)
        for k in (2, 0, 1):
            x_copy(q, k).wait_recv()
            total = total + x2[k, q].astype(f32)
        asum[q] = total.astype(bf16)
        for k in (3, 2, 4, 1, 5, 0, 6):
            a_copy(q, k).start()

    def z_finish(q):
        for way in (0, 1):
            z_copy(q, 4, way).wait_recv()
        total = zbuf[z, q].astype(f32) + z4[0, q].astype(f32) + z4[1, q].astype(f32)
        bsum[q] = total.astype(bf16)
        for k in (1, 0, 2):
            b_copy(q, k).start()

    def adam(q):
        for way in (0, 1):
            y_copy(q, 1, way).wait_recv()
            y_copy(q, 2, way).wait_recv()
        a, first = divmod(q * CW, D)

        def adam_step(i, carry):
            r = pl.ds(pl.multiple_of(i * 16, 16), 16)
            cols = pl.ds(first, CW)
            grad = (
                gbuf[q, y, r, :].astype(f32)
                + y2[0, q, r, :].astype(f32)
                + y2[1, q, r, :].astype(f32)
            )
            if a == 0:
                grad = grad * INV
            m = beta_one * state[2 * a, r, cols] + (1.0 - beta_one) * grad
            v = beta_two * state[2 * a + 1, r, cols] + (1.0 - beta_two) * grad * grad
            old = rows[a, pl.ds(pl.multiple_of(y * OWN + i * 16, 16), 16), cols]
            new = old.astype(f32) - learn_rate * m / (jnp.sqrt(v) + adam_eps)
            (down_ref if a == 0 else up_ref)[r, cols] = new.astype(bf16)
            return carry

        lax.fori_loop(0, OWN // 16, adam_step, 0)

    scale = jnp.where(c == 1, INV, 1.0).astype(f32)

    def finish(q):
        total = asum[q, z].astype(f32)
        for k in range(ZN - 1):
            a_copy(q, k).wait_recv()
            total = total + arecv[q, k].astype(f32)
        fin[q, :, a_tokens] = (total * scale).astype(bf16)
        total = bsum[q, x].astype(f32)
        for k in range(XN - 1):
            b_copy(q, k).wait_recv()
            total = total + brecv[q, k].astype(f32)
        fin[q, :, b_tokens] = (total * scale).astype(bf16)

    z_relay(0, 0)
    z_relay(1, 0)
    z_relay(0, 2)
    z_relay(1, 2)
    y_relay(0)
    y_relay(1)
    z_relay(0, 3)
    z_relay(1, 3)
    x_finish(0)
    y_relay(2)
    y_relay(3)
    x_finish(1)
    z_finish(0)
    z_finish(1)
    for copy in loads[1:]:
        copy.wait()
    adam(0)
    adam(1)
    adam(2)
    finish(0)
    finish(1)
    send_fin.start()
    adam(3)
    mine = fin[c]
    send_fin.wait_recv()
    peer = fpeer[...]
    layer_ref[...] = jnp.where(c == 0, mine, peer)
    input_ref[...] = jnp.where(c == 0, peer, mine)

    send_rows.wait_send()
    send_ws.wait_send()
    send_fin.wait_send()
    for way in (0, 1):
        for q in range(C):
            for kind in range(3):
                y_copy(q, kind, way).wait_send()
        for q in range(Q):
            for kind in range(5):
                z_copy(q, kind, way).wait_send()
    for q in range(Q):
        for k in range(ZN - 1):
            a_copy(q, k).wait_send()
        for k in range(XN - 1):
            x_copy(q, k).wait_send()
            b_copy(q, k).wait_send()


def exchange(coef, rows, tokens, out_grad, dm, dv, um, uv):
    hbm = pl.BlockSpec(memory_space=pltpu.HBM)
    vmem = pl.BlockSpec(memory_space=pltpu.VMEM)
    dma = pltpu.SemaphoreType.DMA
    return pl.pallas_call(
        main_kernel,
        out_shape=(
            pltpu.VMEM((32, T), bf16),
            pltpu.VMEM((32, T), bf16),
            pltpu.VMEM((OWN, D), bf16),
            pltpu.VMEM((OWN, D), bf16),
        ),
        in_specs=[vmem] * 3 + [hbm] * 5,
        out_specs=(vmem,) * 4,
        scratch_shapes=[
            pltpu.VMEM((T, D), bf16),
            pltpu.VMEM((E, D), bf16),
            pltpu.VMEM((2, E, T), bf16),
            pltpu.VMEM((E, T), bf16),
            pltpu.VMEM((4, OWN, D), f32),
            pltpu.VMEM((C, YN, OWN, CW), bf16),
            pltpu.VMEM((2, C, OWN // 2, CW), bf16),
            pltpu.VMEM((2, C, OWN, CW), bf16),
            pltpu.VMEM((XN, Q, ZN, R, TA), bf16),
            pltpu.VMEM((XN - 1, Q, ZN, R, TA), bf16),
            pltpu.VMEM((Q, ZN, R, TA), bf16),
            pltpu.VMEM((2, ZN - 1, R, TA), bf16),
            pltpu.VMEM((ZN, Q, XN, R, TB), bf16),
            pltpu.VMEM((2, Q, XN // 2, R, TB), bf16),
            pltpu.VMEM((2, Q, XN, R, TB), bf16),
            pltpu.VMEM((2, Q, XN, R, TB), bf16),
            pltpu.VMEM((2, Q, XN, R, TB), bf16),
            pltpu.VMEM((Q, XN, R, TB), bf16),
            pltpu.VMEM((2, XN - 1, R, TB), bf16),
            pltpu.VMEM((2, 32, T), bf16),
            pltpu.VMEM((32, T), bf16),
            dma((5,)),
            dma((4,)),
            dma((4,)),
            dma((3, 2, C)),
            dma((3, 2, C)),
            dma((Q, XN - 1)),
            dma((Q, XN - 1)),
            dma((5, 2, Q)),
            dma((5, 2, Q)),
            dma((Q, ZN - 1)),
            dma((Q, ZN - 1)),
            dma((Q, XN - 1)),
            dma((Q, XN - 1)),
        ],
        compiler_params=pltpu.CompilerParams(
            collective_id=0, has_side_effects=True, vmem_limit_bytes=36 * 1024 * 1024
        ),
    )(coef, rows, tokens, out_grad, dm, dv, um, uv)


def write_kernel(*refs):
    copies = [pltpu.make_async_copy(refs[i], refs[4 + i], refs[8].at[i]) for i in range(4)]
    for copy in copies:
        copy.start()
    for copy in copies:
        copy.wait()


def write_out(*arrays):
    return pl.pallas_call(
        write_kernel,
        out_shape=tuple(jax.ShapeDtypeStruct(a.shape, a.dtype) for a in arrays),
        in_specs=[pl.BlockSpec(memory_space=pltpu.VMEM)] * 4,
        out_specs=(pl.BlockSpec(memory_space=pltpu.HBM),) * 4,
        scratch_shapes=[pltpu.SemaphoreType.DMA((4,))],
        compiler_params=pltpu.CompilerParams(vmem_limit_bytes=4 * 1024 * 1024),
    )(*(pltpu.with_memory_space_constraint(a, pltpu.VMEM) for a in arrays))


def local(
    tokens, picks, route_weight, out_grad, down_rows, up_rows, down_mom, down_var, up_mom, up_var
):
    picks_t = picks.transpose(1, 2, 0).reshape(NP, T)
    weight_t = route_weight.transpose(1, 2, 0).reshape(NP, T)
    in_hbm = functools.partial(pltpu.with_memory_space_constraint, memory_space=pltpu.HBM)
    coef, rows, tokens = coefficients(
        *map(in_hbm, (picks_t, weight_t, down_rows, tokens, up_rows))
    )
    layer, grad, new_down, new_up = write_out(*exchange(
        coef, rows, tokens, *map(in_hbm, (out_grad, down_mom, down_var, up_mom, up_var))
    ))
    return (layer.T, grad.T, new_down, new_up)


def solution(mesh):
    placed = (
        P("dp", None),
        P("dp", None, None),
        P("dp", None, None),
        P("dp", None),
        P("expert", None),
        P("expert", None),
        P(("expert", "dp"), None),
        P(("expert", "dp"), None),
        P(("expert", "dp"), None),
        P(("expert", "dp"), None),
    )
    return jax.shard_map(
        local,
        mesh=mesh,
        in_specs=placed,
        out_specs=(
            P("dp", "expert"),
            P("dp", "expert"),
            P(("expert", "dp"), None),
            P(("expert", "dp"), None),
        ),
        check_vma=False,
    )
```

```python
import functools
import math

import jax
import jax.numpy as jnp
from jax import lax
from jax.experimental import pallas as pl
from jax.experimental.pallas import tpu as pltpu
from jax.sharding import PartitionSpec as P

gelu_root = 0.7978845608
gelu_cube = 0.044715
learn_rate = 0.05
beta_one = 0.9
beta_two = 0.999
adam_eps = 1e-08

D = 2048
E = 256
T = 512
NP = 128
OWN = 64
YN, XN, ZN = 4, 4, 8
Q = 2
R = 64 // Q
TA = 256
TB = T - TA
C = 4
CW = 2 * D // C
INV = 1.0 / math.sqrt(D)
MESH = pl.DeviceIdType.MESH
f32 = jnp.float32
bf16 = jnp.bfloat16


def coefficient_kernel(
    picks_hbm, weight_hbm, down_hbm, tok_hbm, up_hbm,
    coef_ref, rows_ref, acts_ref, key_ref, weight_ref, sem,
):
    loads = []
    for i, (src, dst) in enumerate((
        (picks_hbm, key_ref), (weight_hbm, weight_ref),
        (down_hbm, rows_ref.at[0]), (tok_hbm, acts_ref),
        (up_hbm, rows_ref.at[1]),
    )):
        copy = pltpu.make_async_copy(src, dst, sem.at[i])
        copy.start()
        loads.append(copy)
    coef_ref[...] = jnp.zeros((E, T), f32)
    loads[0].wait()
    first = lax.axis_index("expert") * E
    key = key_ref[...] - first
    own = jnp.logical_and(key >= 0, key < E)
    key_ref[...] = jnp.where(own, key, -1)
    rounds = jnp.max(jnp.sum(own.astype(jnp.int32), axis=0, keepdims=True))
    loads[1].wait()

    def one_round(_, last):
        keys = key_ref[...]
        now = jnp.max(jnp.where(keys < last, keys, -1), axis=0, keepdims=True)
        total = jnp.sum(
            jnp.where(keys == now, weight_ref[...], 0.0), axis=0, keepdims=True
        )
        ids = lax.broadcasted_iota(jnp.int32, (E, T), 0)
        coef_ref[...] = jnp.where(ids == now, total, coef_ref[...])
        return now

    lax.fori_loop(0, rounds, one_round, jnp.full((1, T), E, jnp.int32))
    for copy in loads[2:]:
        copy.wait()


def coefficients(picks, weights, down_rows, tokens, up_rows):
    vmem = pl.BlockSpec(memory_space=pltpu.VMEM)
    hbm = pl.BlockSpec(memory_space=pltpu.HBM)
    return pl.pallas_call(
        coefficient_kernel,
        out_shape=(
            pltpu.VMEM((E, T), f32),
            pltpu.VMEM((2, E, D), bf16),
            pltpu.VMEM((T, D), bf16),
        ),
        in_specs=[hbm] * 5,
        out_specs=(vmem, vmem, vmem),
        scratch_shapes=[
            pltpu.VMEM((NP, T), jnp.int32),
            pltpu.VMEM((NP, T), f32),
            pltpu.SemaphoreType.DMA((5,)),
        ],
        compiler_params=pltpu.CompilerParams(vmem_limit_bytes=24 * 1024 * 1024),
    )(picks, weights, down_rows, tokens, up_rows)


def main_kernel(
    coef, rows, tok, cot_hbm, dm_hbm, dv_hbm, um_hbm, uv_hbm,
    layer_ref, input_ref, down_ref, up_ref,
    cot, prow, ws, pws, state,
    gbuf, y1, y2, xbuf, x2, asum, arecv,
    zbuf, z1, z2, z3, z4, bsum, brecv, fin, fpeer,
    load_sem, pair_send, pair_recv, y_send, y_recv, x_send, x_recv,
    z_send, z_recv, a_send, a_recv, b_send, b_recv,
):
    y = lax.axis_index("dp")
    e = lax.axis_index("expert")
    c = lax.rem(e, 2)
    z = lax.rem(e // 2, ZN)
    x = e // (2 * ZN)

    def at(xx, zz, cc=c):
        return (y, (xx * ZN + zz) * 2 + cc)

    def xat(k):
        return lax.rem(x + k + XN, XN)

    def zat(k):
        return lax.rem(z + k + ZN, ZN)

    def yat(k):
        return lax.rem(y + k + YN, YN)

    sibling = (y, (x * ZN + z) * 2 + 1 - c)

    loads = []
    for i, (src, dst) in enumerate((
        (cot_hbm, cot), (dm_hbm, state.at[0]), (dv_hbm, state.at[1]),
        (um_hbm, state.at[2]), (uv_hbm, state.at[3]),
    )):
        copy = pltpu.make_async_copy(src, dst, load_sem.at[i])
        copy.start()
        loads.append(copy)

    barrier = pltpu.get_barrier_semaphore()
    greet = [sibling, (yat(1), e), (yat(-1), e)]
    for cc in (c,):
        greet += [at(xat(k), z, cc) for k in range(1, XN)]
        greet += [at(x, zat(k), cc) for k in range(1, ZN)]
    for who in greet:
        pl.semaphore_signal(barrier, inc=1, device_id=who, device_id_type=MESH)

    def remote(src, dst, send, recv, who):
        return pltpu.make_async_remote_copy(
            src_ref=src, dst_ref=dst, send_sem=send, recv_sem=recv,
            device_id=who, device_id_type=MESH,
        )

    def y_copy(q, kind, way):
        low = (kind != 1) == (way == 0)
        near = 1 if way == 0 else -1
        block = yat(2 if kind == 0 else near)
        half = pl.ds(0 if low else OWN // 2, OWN // 2)
        src = gbuf.at[q, block, half, :]
        dst = y1.at[way, q] if kind == 0 else y2.at[way, q, half, :]
        sems = y_send.at[kind, way, q], y_recv.at[kind, way, q]
        return remote(src, dst, *sems, (yat(near), e))

    def x_copy(q, k):
        p = xat(k + 1)
        sems = x_send.at[q, k], x_recv.at[q, k]
        return remote(xbuf.at[p, q], x2.at[k, q], *sems, at(p, z))

    def z_copy(q, kind, way):
        low = (kind != 1) == (way == 0)
        near = 1 if way == 0 else -1
        block = zat((4, 3, 3, 2, 1)[kind] * near)
        half = pl.ds(0 if low else XN // 2, XN // 2)
        src = zbuf.at[block, q] if kind > 2 else zbuf.at[block, q, half]
        if kind == 0:
            dst = z1.at[way, q]
        elif kind < 3:
            dst = z2.at[way, q, half]
        else:
            dst = (z3 if kind == 3 else z4).at[way, q]
        sems = z_send.at[kind, way, q], z_recv.at[kind, way, q]
        return remote(src, dst, *sems, at(x, zat(near)))

    def a_copy(q, k):
        p = zat(k + 1)
        sems = a_send.at[q, k], a_recv.at[q, k]
        return remote(asum.at[q, p], arecv.at[q, k], *sems, at(x, p))

    def b_copy(q, k):
        p = xat(k + 1)
        sems = b_send.at[q, k], b_recv.at[q, k]
        return remote(bsum.at[q, p], brecv.at[q, k], *sems, at(p, z))

    def pair_copy(i, src, dst):
        return remote(src, dst, pair_send.at[i], pair_recv.at[i], sibling)

    send_rows = pair_copy(0, rows.at[c], prow)
    send_ws = pair_copy(1, ws.at[c], pws)
    send_fin = pair_copy(2, fin.at[1 - c], fpeer)

    s = lax.dot_general(
        rows[0], tok[...], (((1,), (1,)), ((), ())), preferred_element_type=f32
    ) * INV
    pl.semaphore_wait(barrier, len(greet))
    send_rows.start()
    loads[0].wait()
    b = lax.dot_general(
        rows[1], cot[...], (((1,), (1,)), ((), ())), preferred_element_type=f32
    )
    k = coef[...]
    u = jnp.tanh(gelu_root * (s + gelu_cube * s * s * s))
    ws[1] = (k * (0.5 * s * (1.0 + u))).astype(bf16)
    slope = 0.5 * (1.0 + u) + 0.5 * s * (1.0 - u * u) * gelu_root * (
        1.0 + 3.0 * gelu_cube * s * s
    )
    ws[0] = (k * slope * b).astype(bf16)
    send_ws.start()

    def gradients(q):
        a, first = divmod(q * CW, D)
        g = jnp.dot(
            ws[a], (tok, cot)[a][:, first : first + CW], preferred_element_type=f32
        )
        gbuf[q] = g.astype(bf16).reshape(YN, OWN, CW)
        for kind in (0, 1) if q == 0 else (0,):
            for way in (0, 1):
                y_copy(q, kind, way).start()

    def partial_rows(block, tokens):
        cols = pl.ds(pl.multiple_of(block * 512, 512), 512)
        part = lax.dot_general(
            rows[1 - c, :, cols], ws[1 - c, :, tokens], (((0,), (0,)), ((), ())),
            preferred_element_type=f32,
        ) + lax.dot_general(
            prow[:, cols], pws[:, tokens], (((0,), (0,)), ((), ())),
            preferred_element_type=f32,
        )
        return part.astype(bf16)

    a_tokens, b_tokens = slice(0, TA), slice(TA, T)

    gradients(0)
    send_rows.wait_recv()
    send_ws.wait_recv()
    for i in range(XN):
        part = partial_rows(i, b_tokens)
        for j in range(ZN):
            for q in range(Q):
                r = j * 64 + q * R
                zbuf[j, q, i] = part[r : r + R, :]
    for q in range(Q):
        for way in (0, 1):
            z_copy(q, 0, way).start()
    for way in (0, 1):
        z_copy(0, 1, way).start()
    for step in (2, 1, -1, 0):
        block = xat(step)
        part = partial_rows(block, a_tokens)
        for j in range(ZN):
            for q in range(Q):
                r = j * 64 + q * R
                xbuf[block, q, j] = part[r : r + R, :]
        if step:
            x_copy(0, step - 1 if step > 0 else 2).start()
        if step == -1:
            for k in (1, 0, 2):
                x_copy(1, k).start()
            gradients(1)
    gradients(2)
    gradients(3)
    for way in (0, 1):
        y_copy(1, 1, way).start()

    def z_relay(q, kind):
        for way in (0, 1):
            near = 1 if way == 0 else -1
            if kind == 0:
                z_copy(q, 0, way).wait_recv()
                block = zat(3 * near)
                half = pl.ds(0 if way == 0 else XN // 2, XN // 2)
                mine = zbuf[block, q, half].astype(f32)
                zbuf[block, q, half] = (mine + z1[way, q].astype(f32)).astype(bf16)
                z_copy(q, 2, way).start()
                if q + 1 < Q:
                    z_copy(q + 1, 1, way).start()
            else:
                if kind == 2:
                    z_copy(q, 1, way).wait_recv()
                z_copy(q, kind, way).wait_recv()
                block = zat((2 if kind == 2 else 1) * near)
                got = (z2 if kind == 2 else z3)[way, q].astype(f32)
                zbuf[block, q] = (zbuf[block, q].astype(f32) + got).astype(bf16)
                z_copy(q, kind + 1, way).start()

    def y_relay(q):
        for way in (0, 1):
            y_copy(q, 0, way).wait_recv()
            block = yat(1 if way == 0 else -1)
            half = pl.ds(0 if way == 0 else OWN // 2, OWN // 2)
            mine = gbuf[q, block, half, :].astype(f32)
            gbuf[q, block, half, :] = (mine + y1[way, q].astype(f32)).astype(bf16)
            y_copy(q, 2, way).start()
            if q + 2 < C:
                y_copy(q + 2, 1, way).start()

    def x_finish(q):
        total = xbuf[x, q].astype(f32)
        for k in (2, 0, 1):
            x_copy(q, k).wait_recv()
            total = total + x2[k, q].astype(f32)
        asum[q] = total.astype(bf16)
        for k in (3, 2, 4, 1, 5, 0, 6):
            a_copy(q, k).start()

    def z_finish(q):
        for way in (0, 1):
            z_copy(q, 4, way).wait_recv()
        total = zbuf[z, q].astype(f32) + z4[0, q].astype(f32) + z4[1, q].astype(f32)
        bsum[q] = total.astype(bf16)
        for k in (1, 0, 2):
            b_copy(q, k).start()

    def adam(q):
        for way in (0, 1):
            y_copy(q, 1, way).wait_recv()
            y_copy(q, 2, way).wait_recv()
        a, first = divmod(q * CW, D)

        def adam_step(i, carry):
            r = pl.ds(pl.multiple_of(i * 16, 16), 16)
            cols = pl.ds(first, CW)
            grad = (
                gbuf[q, y, r, :].astype(f32)
                + y2[0, q, r, :].astype(f32)
                + y2[1, q, r, :].astype(f32)
            )
            if a == 0:
                grad = grad * INV
            m = beta_one * state[2 * a, r, cols] + (1.0 - beta_one) * grad
            v = beta_two * state[2 * a + 1, r, cols] + (1.0 - beta_two) * grad * grad
            old = rows[a, pl.ds(pl.multiple_of(y * OWN + i * 16, 16), 16), cols]
            new = old.astype(f32) - learn_rate * m / (jnp.sqrt(v) + adam_eps)
            (down_ref if a == 0 else up_ref)[r, cols] = new.astype(bf16)
            return carry

        lax.fori_loop(0, OWN // 16, adam_step, 0)

    scale = jnp.where(c == 1, INV, 1.0).astype(f32)

    def finish(q):
        total = asum[q, z].astype(f32)
        for k in range(ZN - 1):
            a_copy(q, k).wait_recv()
            total = total + arecv[q, k].astype(f32)
        fin[q, :, a_tokens] = (total * scale).astype(bf16)
        total = bsum[q, x].astype(f32)
        for k in range(XN - 1):
            b_copy(q, k).wait_recv()
            total = total + brecv[q, k].astype(f32)
        fin[q, :, b_tokens] = (total * scale).astype(bf16)

    z_relay(0, 0)
    z_relay(1, 0)
    z_relay(0, 2)
    z_relay(1, 2)
    y_relay(0)
    y_relay(1)
    z_relay(0, 3)
    z_relay(1, 3)
    x_finish(0)
    y_relay(2)
    y_relay(3)
    x_finish(1)
    z_finish(0)
    z_finish(1)
    for copy in loads[1:]:
        copy.wait()
    adam(0)
    adam(1)
    finish(1 - c)
    send_fin.start()
    finish(c)
    adam(2)
    adam(3)
    mine = fin[c]
    send_fin.wait_recv()
    peer = fpeer[...]
    layer_ref[...] = jnp.where(c == 0, mine, peer)
    input_ref[...] = jnp.where(c == 0, peer, mine)

    send_rows.wait_send()
    send_ws.wait_send()
    send_fin.wait_send()
    for way in (0, 1):
        for q in range(C):
            for kind in range(3):
                y_copy(q, kind, way).wait_send()
        for q in range(Q):
            for kind in range(5):
                z_copy(q, kind, way).wait_send()
    for q in range(Q):
        for k in range(ZN - 1):
            a_copy(q, k).wait_send()
        for k in range(XN - 1):
            x_copy(q, k).wait_send()
            b_copy(q, k).wait_send()


def exchange(coef, rows, tokens, out_grad, dm, dv, um, uv):
    hbm = pl.BlockSpec(memory_space=pltpu.HBM)
    vmem = pl.BlockSpec(memory_space=pltpu.VMEM)
    dma = pltpu.SemaphoreType.DMA
    return pl.pallas_call(
        main_kernel,
        out_shape=(
            pltpu.VMEM((32, T), bf16),
            pltpu.VMEM((32, T), bf16),
            pltpu.VMEM((OWN, D), bf16),
            pltpu.VMEM((OWN, D), bf16),
        ),
        in_specs=[vmem] * 3 + [hbm] * 5,
        out_specs=(vmem,) * 4,
        scratch_shapes=[
            pltpu.VMEM((T, D), bf16),
            pltpu.VMEM((E, D), bf16),
            pltpu.VMEM((2, E, T), bf16),
            pltpu.VMEM((E, T), bf16),
            pltpu.VMEM((4, OWN, D), f32),
            pltpu.VMEM((C, YN, OWN, CW), bf16),
            pltpu.VMEM((2, C, OWN // 2, CW), bf16),
            pltpu.VMEM((2, C, OWN, CW), bf16),
            pltpu.VMEM((XN, Q, ZN, R, TA), bf16),
            pltpu.VMEM((XN - 1, Q, ZN, R, TA), bf16),
            pltpu.VMEM((Q, ZN, R, TA), bf16),
            pltpu.VMEM((2, ZN - 1, R, TA), bf16),
            pltpu.VMEM((ZN, Q, XN, R, TB), bf16),
            pltpu.VMEM((2, Q, XN // 2, R, TB), bf16),
            pltpu.VMEM((2, Q, XN, R, TB), bf16),
            pltpu.VMEM((2, Q, XN, R, TB), bf16),
            pltpu.VMEM((2, Q, XN, R, TB), bf16),
            pltpu.VMEM((Q, XN, R, TB), bf16),
            pltpu.VMEM((2, XN - 1, R, TB), bf16),
            pltpu.VMEM((2, 32, T), bf16),
            pltpu.VMEM((32, T), bf16),
            dma((5,)),
            dma((4,)),
            dma((4,)),
            dma((3, 2, C)),
            dma((3, 2, C)),
            dma((Q, XN - 1)),
            dma((Q, XN - 1)),
            dma((5, 2, Q)),
            dma((5, 2, Q)),
            dma((Q, ZN - 1)),
            dma((Q, ZN - 1)),
            dma((Q, XN - 1)),
            dma((Q, XN - 1)),
        ],
        compiler_params=pltpu.CompilerParams(
            collective_id=0, has_side_effects=True, vmem_limit_bytes=36 * 1024 * 1024
        ),
    )(coef, rows, tokens, out_grad, dm, dv, um, uv)


def write_kernel(*refs):
    copies = [pltpu.make_async_copy(refs[i], refs[4 + i], refs[8].at[i]) for i in range(4)]
    for copy in copies:
        copy.start()
    for copy in copies:
        copy.wait()


def write_out(*arrays):
    return pl.pallas_call(
        write_kernel,
        out_shape=tuple(jax.ShapeDtypeStruct(a.shape, a.dtype) for a in arrays),
        in_specs=[pl.BlockSpec(memory_space=pltpu.VMEM)] * 4,
        out_specs=(pl.BlockSpec(memory_space=pltpu.HBM),) * 4,
        scratch_shapes=[pltpu.SemaphoreType.DMA((4,))],
        compiler_params=pltpu.CompilerParams(vmem_limit_bytes=4 * 1024 * 1024),
    )(*(pltpu.with_memory_space_constraint(a, pltpu.VMEM) for a in arrays))


def local(
    tokens, picks, route_weight, out_grad, down_rows, up_rows, down_mom, down_var, up_mom, up_var
):
    picks_t = picks.transpose(1, 2, 0).reshape(NP, T)
    weight_t = route_weight.transpose(1, 2, 0).reshape(NP, T)
    in_hbm = functools.partial(pltpu.with_memory_space_constraint, memory_space=pltpu.HBM)
    coef, rows, tokens = coefficients(
        *map(in_hbm, (picks_t, weight_t, down_rows, tokens, up_rows))
    )
    layer, grad, new_down, new_up = write_out(*exchange(
        coef, rows, tokens, *map(in_hbm, (out_grad, down_mom, down_var, up_mom, up_var))
    ))
    return (layer.T, grad.T, new_down, new_up)


def solution(mesh):
    placed = (
        P("dp", None),
        P("dp", None, None),
        P("dp", None, None),
        P("dp", None),
        P("expert", None),
        P("expert", None),
        P(("expert", "dp"), None),
        P(("expert", "dp"), None),
        P(("expert", "dp"), None),
        P(("expert", "dp"), None),
    )
    return jax.shard_map(
        local,
        mesh=mesh,
        in_specs=placed,
        out_specs=(
            P("dp", "expert"),
            P("dp", "expert"),
            P(("expert", "dp"), None),
            P(("expert", "dp"), None),
        ),
        check_vma=False,
    )
```
